32 devices in a mesh: seq: 8 (over z, x), batch: 4 (over y, core).
Axes of the slice: x: 2, y: 2, z: 4, core: 2. Of those that a mesh axis runs over, the one named last changes fastest.
Arguments:
- events: bfloat16 [4, 32768, 1, 256], P('batch', 'seq'), may hold values from -6 to 6
- spectral_filter: float32 [2, 32768, 256], P(None, None, 'seq'), may hold values from -6 to 6
- ln_gain: float32 [256], replicated, may hold values from 0.1 to 1.9
- w_in: bfloat16 [64, 1024, 256], P('seq', 'batch'), may hold values from -0.375 to 0.375
- w_out: bfloat16 [64, 1024, 256], P('seq', 'batch'), may hold values from -0.1875 to 0.1875
- gate_weight: bfloat16 [3, 256, 64], replicated, may hold values from -0.375 to 0.375
- gate_table: float32 [3, 16], replicated, may hold values from -4 to 4
- routes: int32 [4, 32768, 1, 1], P('batch', 'seq'), may hold values from 0 to 63; in each aligned block of 4096 rows (0 to 4095, 4096 to 8191, ..., all dimensions but the last counted through in order) at most 128 rows name the same one
- gate_index: int32 [4, 32768, 1, 3], P('batch', 'seq'), may hold values from 0 to 15
Outputs:
- task_out: bfloat16 [3, 4, 32768, 1, 256], P(None, 'batch', 'seq')
The draws below stay inside these ranges and needn't reach their ends.
Inputs may be any that keep to these rules, and one draw needn't show every extreme that they name: `routes`: in each aligned block of 4096 rows (the events of one device) no expert is named by more than 128 rows; in some block one expert is named by exactly 128.
All inputs are finite; a program needn't handle non-finite values.
Results may differ from the reference program's by a relative error of at most 0.0072.
Values may be sent and summed in bfloat16 or wider, within the bound.
A program may use at most 128 MiB of HBM per device.

```python
import math
import jax
import jax.numpy as jnp
import numpy as np
from jax import lax

C = 256
L = 32768
HID = 1024
EXPERTS = 64
TASKS = 3
GATE_ROWS = 16
USERS_DEV = 1
GROUPS = 4
TOK_DEV = 4096
CAP = 128


def set_ends(entries, key, smallest, high):
    shape = entries.shape
    spot = [jax.random.randint(jax.random.fold_in(key, axis), (), 0, shape[axis]) for axis in range(len(shape))]
    entries = entries.at[tuple(spot)].set(smallest)
    longest = shape.index(max(shape))
    spot[longest] = (spot[longest] + 1) % shape[longest]
    return entries.at[tuple(spot)].set(high)


def block_levels(rng, extent, pieces, low, top_value):
    factor_of, own = 1.0, jax.random.fold_in(rng, 6)
    for axis_at, shards_of in pieces:
        draws = jnp.exp(jax.random.uniform(jax.random.fold_in(own, axis_at), (shards_of,), jnp.float32, low / len(pieces), top_value / len(pieces)))
        factor_of = factor_of * jnp.repeat(draws, extent[axis_at] // shards_of).reshape([-1 if axis == axis_at else 1 for axis in range(len(extent))])
    return factor_of


def deal_out(stream_key, own, number, rows, number_of, top, bound, slope):
    ranking = jax.random.permutation(stream_key, number_of)
    heavy_load, ordinary = load_shares(number_of, rows * top, bound, slope, True), load_shares(number_of, rows * top, bound, slope, False)
    places = jnp.arange(number_of)

    def named(tallies, rotation):
        used = int((tallies > 0).sum())
        fixed = max(1, used // 4)
        passed = fixed + (places - fixed + rotation * (used - fixed)) % max(1, number_of - fixed)
        return jnp.zeros((number_of,), jnp.int32).at[ranking[jnp.where(places < fixed, places, passed)]].set(jnp.asarray(tallies, jnp.int32))

    tallies = jnp.where(number % 4 == 0, named(heavy_load, number // 4), named(ordinary, number - number // 4 - 1))
    mixed = jax.random.permutation(jax.random.fold_in(own, 3), number_of)
    donor, receiver = mixed[0:number_of // 2 * 2:2], mixed[1:number_of // 2 * 2:2]
    slack = jnp.minimum(tallies[donor] - 1, bound - tallies[receiver]) // 2
    slack = jnp.where((donor == ranking[0]) | (receiver == ranking[0]) | (tallies[receiver] == 0), 0, jnp.maximum(slack, 0))
    passed = jax.random.randint(jax.random.fold_in(own, 4), (number_of // 2,), 0, 1 << 20) % (slack + 1)
    tallies = tallies.at[donor].add(-passed).at[receiver].add(passed)
    items = jnp.searchsorted(jnp.cumsum(tallies), jnp.arange(rows * top), side="right").astype(jnp.int32)
    listing = items.reshape(top, rows).T
    listing = listing[jax.random.permutation(jax.random.fold_in(own, 1), rows)]
    rotation = jax.random.randint(jax.random.fold_in(own, 2), (rows, 1), 0, top)
    return jnp.take_along_axis(listing, (jnp.arange(top)[None, :] + rotation) % top, axis=1)


def load_shares(amount, total, reach, skew, full):
    weights = [(1 << 20) // math.isqrt(grade ** skew) + 1 for grade in range(1, amount + 1)]
    largest = reach if full else min(reach, max(-(-total // amount), total * weights[0] // sum(weights)))
    least = 1 if total - largest >= amount - 1 else 0
    given, spare = [largest] + [least] * (amount - 1), total - largest - least * (amount - 1)
    while spare > 0:
        free = [i for i in range(1, amount) if given[i] < largest] or [i for i in range(1, amount) if given[i] < reach]
        whole, remaining = sum([weights[i] for i in free]), spare
        for i in free:
            addition = min(reach - given[i], max(1, remaining * weights[i] // whole), spare)
            given[i] = given[i] + addition
            spare = spare - addition
    return np.array(given)


def noise(own_key, dims, spread, most, shards=(), kind=jnp.bfloat16):
    drawn = spread * jax.random.normal(own_key, dims, jnp.float32)
    if shards:
        drawn = drawn * block_levels(own_key, dims, shards, -0.22, 0.18)
    return jnp.clip(drawn, -most, most).astype(kind)


def setup_inputs(seed: int = 0) -> dict:
    key_list = jax.random.split(jax.random.key(seed), 10)
    events = noise(key_list[0], (GROUPS, L, USERS_DEV, C), 1.0, 6.0, ((0, 4), (1, 8)))
    spectral_filter = noise(key_list[1], (2, L, C), 1.0, 6.0, ((2, 8),), jnp.float32)
    ln_gain = jnp.clip(1.0 + 0.18 * jax.random.normal(key_list[2], (C,), jnp.float32), 0.1, 1.9)
    w_in = noise(key_list[3], (EXPERTS, HID, C), C ** -0.5, 0.375, ((0, 8), (1, 4)))
    w_out = noise(key_list[4], (EXPERTS, HID, C), HID ** -0.5, 0.1875, ((0, 8), (1, 4)))
    gate_weight = noise(key_list[5], (TASKS, C, EXPERTS), C ** -0.5, 0.375)
    gate_table = noise(key_list[6], (TASKS, GATE_ROWS), 1.0, 4.0, (), jnp.float32)
    routes_keys = jax.random.split(jax.random.fold_in(key_list[7], 1), GROUPS * L * USERS_DEV // TOK_DEV)
    routes_turns = jax.random.permutation(jax.random.fold_in(key_list[7], 3), GROUPS * L * USERS_DEV // TOK_DEV)
    routes = jax.vmap(lambda own, number: deal_out(jax.random.fold_in(key_list[7], 2), own, number, TOK_DEV, EXPERTS, 1, CAP, 2))(routes_keys, routes_turns).reshape((GROUPS, L, USERS_DEV, 1))
    gate_index = set_ends(jax.random.randint(key_list[8], (GROUPS, L, USERS_DEV, TASKS), 0, GATE_ROWS), jax.random.fold_in(key_list[8], 1), 0, GATE_ROWS - 1).astype(jnp.int32)
    return dict(events=events, spectral_filter=spectral_filter, ln_gain=ln_gain, w_in=w_in, w_out=w_out, gate_weight=gate_weight, gate_table=gate_table, routes=routes, gate_index=gate_index)


def layer_norm(summed, gain_vec):
    centre = lax.optimization_barrier(jnp.mean(summed, -1, keepdims=True))
    spread_sq = lax.optimization_barrier(jnp.mean(jnp.square(summed - centre), -1, keepdims=True))
    return ((summed - centre) * lax.rsqrt(spread_sq + 1e-05) * gain_vec).astype(jnp.bfloat16)

def reference(events, spectral_filter, ln_gain, w_in, w_out, gate_weight, gate_table, routes, gate_index):
    filter_full = lax.complex(spectral_filter[0], spectral_filter[1])

    def filter_one(sequence):
        values = sequence.astype(jnp.float32)
        spectrum = jnp.fft.fft(values, axis=0)
        filtered = jnp.real(jnp.fft.ifft(spectrum * filter_full, axis=0)).astype(jnp.float32)
        return (values + filtered).astype(jnp.bfloat16)
    histories = jnp.transpose(events, (0, 2, 1, 3)).reshape(GROUPS * USERS_DEV, L, C)
    summed = lax.map(filter_one, histories).reshape(GROUPS, USERS_DEV, L, C).transpose(0, 2, 1, 3)
    normed = layer_norm(summed.astype(jnp.float32), ln_gain).reshape(-1, C)
    expert_ids = routes.reshape(-1).astype(jnp.int32)
    row_total = expert_ids.shape[0]
    sort_order = jnp.argsort(expert_ids, stable=True).astype(jnp.int32)
    block_rows = math.gcd(row_total, 512)
    sorted_rows = normed[sort_order].reshape(-1, block_rows, C)
    sorted_ids = expert_ids[sort_order].reshape(-1, block_rows)
    gate_cols = gate_weight.transpose(1, 0, 2).reshape(C, TASKS * EXPERTS)

    def run_block(pair):
        rows, block_ids = pair

        def apply_one(expert, current):
            hidden = jnp.maximum(jnp.dot(rows, w_in[expert].T, preferred_element_type=jnp.float32), 0.0).astype(jnp.bfloat16)
            output = jnp.dot(hidden, w_out[expert], preferred_element_type=jnp.float32)
            return jnp.where((block_ids == expert)[:, None], output, current)
        initial = jnp.zeros((block_rows, C), jnp.float32)
        expert_out = lax.fori_loop(block_ids[0], block_ids[-1] + 1, apply_one, initial).astype(jnp.bfloat16)
        scores = jnp.dot(rows, gate_cols, preferred_element_type=jnp.float32).reshape(block_rows, TASKS, EXPERTS)
        chosen = jnp.take_along_axis(scores, block_ids[:, None, None], axis=2)[:, :, 0].astype(jnp.bfloat16)
        return (expert_out, chosen)
    out_sorted, chosen_sorted = lax.map(run_block, (sorted_rows, sorted_ids))
    expert_rows = jnp.zeros((row_total, C), jnp.bfloat16).at[sort_order].set(out_sorted.reshape(row_total, C))
    chosen = jnp.zeros((row_total, TASKS), jnp.bfloat16).at[sort_order].set(chosen_sorted.reshape(row_total, TASKS))
    lookup = gate_index.reshape(row_total, TASKS)
    table_bias = gate_table[jnp.arange(TASKS, dtype=jnp.int32)[None, :], lookup]
    gate_vals = jax.nn.sigmoid(chosen.astype(jnp.float32) + table_bias)
    task_out = (gate_vals.T[:, :, None] * expert_rows.astype(jnp.float32)[None]).astype(jnp.bfloat16)
    return task_out.reshape(TASKS, GROUPS, L, USERS_DEV, C)
```

```python
import functools
import math

import jax
import jax.numpy as jnp
import numpy as np
from jax import lax
from jax.experimental import pallas as pl
from jax.experimental.pallas import tpu as pltpu
from jax.sharding import PartitionSpec as P

EXPERTS = 64
TASKS = 3
INNER = 256
LANES = 128
VMEM_BYTES = 56 * 2**20
F32 = jnp.float32
BF16 = jnp.bfloat16


def params():
    return pltpu.CompilerParams(vmem_limit_bytes=VMEM_BYTES)


def dot_nt(a, b):
    return lax.dot_general(a, b, (((1,), (1,)), ((), ())), preferred_element_type=F32)


def dot_nn(a, b):
    return jnp.dot(a, b, preferred_element_type=F32)


def tables(length):
    outer = length // INNER

    def angles(rows, cols, points):
        product = np.outer(np.arange(rows), np.arange(cols)) % points
        return product * (2.0 * np.pi / points)

    first = angles(outer, outer, outer)
    inner = angles(INNER, INNER, INNER)
    turn = angles(outer, INNER, length)
    c1, s1, c2, s2 = np.cos(first), np.sin(first), np.cos(inner), np.sin(inner)
    f1 = np.concatenate([c1, -s1], 0)
    m2 = np.block([[c2, s2], [-s2, c2]])
    m3 = np.block([[c2, -s2], [s2, c2]])
    f4 = np.concatenate([c1, -s1], 1) / length
    bf = lambda a: jnp.asarray(a.astype(np.float32)).astype(BF16)
    fl = lambda a: jnp.asarray(a.astype(np.float32))
    return (
        bf(f1), bf(m2), bf(m3), bf(f4),
        fl(np.cos(turn)), fl(np.sin(turn)), fl(np.cos(turn).T), fl(np.sin(turn).T),
    )


def turn_kernel(blocks, x_ref, out_ref, low, high):
    def step(j, _):
        rows = x_ref[pl.ds(pl.multiple_of(j * INNER, INNER), INNER), :]
        turned = rows.astype(F32).T
        low[pl.ds(j, LANES, stride=blocks), :] = turned[:, :LANES]
        high[pl.ds(j, LANES, stride=blocks), :] = turned[:, LANES:]
        return 0

    lax.fori_loop(0, blocks, step, 0, unroll=2)
    out_ref[:, :LANES] = low[...].astype(BF16)
    out_ref[:, LANES:] = high[...].astype(BF16)


def turn(events):
    tokens, channels = events.shape
    blocks = tokens // INNER
    rows = LANES * blocks
    return pl.pallas_call(
        functools.partial(turn_kernel, blocks),
        grid=(channels // LANES,),
        in_specs=[pl.BlockSpec((tokens, LANES), lambda i: (0, i))],
        out_specs=pl.BlockSpec((rows, INNER), lambda i: (i, 0)),
        out_shape=jax.ShapeDtypeStruct((channels * blocks, INNER), BF16),
        scratch_shapes=[pltpu.VMEM((rows, LANES), F32), pltpu.VMEM((rows, LANES), F32)],
        compiler_params=params(),
        name="turn",
    )(events)


def spectral_kernel(
    chans, outer, x_ref, h_ref, f1_ref, m2_ref, m3_ref, f4_ref, tc, ts, tct, tst, out_ref,
    y_ref, g_ref,
):
    x_all = x_ref[...]
    for c in range(chans):
        x = x_all[:, c].reshape(outer, INNER)
        a = dot_nn(f1_ref[...], x)
        re, im = a[:outer], a[outer:]
        rows = slice(c * outer, (c + 1) * outer)
        y_ref[rows, :INNER] = (re * tc[...] + im * ts[...]).astype(BF16)
        y_ref[rows, INNER:] = (im * tc[...] - re * ts[...]).astype(BF16)
    z = dot_nt(m2_ref[...], y_ref[...])
    for c in range(chans):
        cols = slice(c * outer, (c + 1) * outer)
        zr, zi = z[:INNER, cols], z[INNER:, cols]
        hr, hi = h_ref[0, c], h_ref[1, c]
        g_ref[:INNER, cols] = (zr * hr - zi * hi).astype(BF16)
        g_ref[INNER:, cols] = (zr * hi + zi * hr).astype(BF16)
    u = dot_nn(m3_ref[...], g_ref[...])
    for c in range(chans):
        cols = slice(c * outer, (c + 1) * outer)
        ur, ui = u[:INNER, cols], u[INNER:, cols]
        v = jnp.concatenate(
            [
                (ur * tct[...] - ui * tst[...]).astype(BF16),
                (ui * tct[...] + ur * tst[...]).astype(BF16),
            ],
            1,
        )
        y = dot_nt(f4_ref[...], v)
        x = x_all[:, c].reshape(outer, INNER)
        total = (x.astype(F32) + y).astype(BF16)
        out_ref[:, c] = total.reshape(out_ref.shape[0], out_ref.shape[2], INNER)


def spectral(x, spectral_filter):
    parts, chan_dev, blocks, _ = x.shape
    length = parts * blocks * INNER
    outer = length // INNER
    chans = math.gcd(chan_dev, 4)
    consts = tables(length)
    filt = spectral_filter.transpose(0, 2, 1).reshape(2, chan_dev, INNER, outer)
    whole = lambda a: pl.BlockSpec(a.shape, lambda i: (0,) * a.ndim)
    x_spec = pl.BlockSpec((parts, chans, blocks, INNER), lambda i: (0, i, 0, 0))
    return pl.pallas_call(
        functools.partial(spectral_kernel, chans, outer),
        grid=(chan_dev // chans,),
        in_specs=[x_spec, pl.BlockSpec((2, chans, INNER, outer), lambda i: (0, i, 0, 0))]
        + [whole(a) for a in consts],
        out_specs=x_spec,
        out_shape=jax.ShapeDtypeStruct(x.shape, BF16),
        scratch_shapes=[
            pltpu.VMEM((chans * outer, 2 * INNER), BF16),
            pltpu.VMEM((2 * INNER, chans * outer), BF16),
        ],
        compiler_params=params(),
        name="spectral",
    )(x, filt, *consts)


def slot_kernel(capacity, routes_ref, slot_ref):
    tokens = routes_ref.shape[1]
    row = lax.broadcasted_iota(jnp.int32, (INNER, INNER), 0)
    col = lax.broadcasted_iota(jnp.int32, (INNER, INNER), 1)
    before = (row < col).astype(F32).astype(BF16)
    expert = lax.broadcasted_iota(jnp.int32, (EXPERTS, INNER), 0)
    base = (lax.broadcasted_iota(jnp.int32, (EXPERTS, 1), 0) * capacity).astype(F32)
    for j in range(tokens // INNER):
        cols = slice(j * INNER, (j + 1) * INNER)
        hot = (expert == routes_ref[:, cols]).astype(F32)
        rank = dot_nn(hot.astype(BF16), before)
        slot_ref[:, cols] = jnp.sum(hot * (rank + base), 0, keepdims=True).astype(jnp.int32)
        base = base + jnp.sum(hot, 1, keepdims=True)


def slots_of(routes, capacity):
    return pl.pallas_call(
        functools.partial(slot_kernel, capacity),
        out_shape=jax.ShapeDtypeStruct(routes.shape, jnp.int32),
        compiler_params=params(),
        name="slots",
    )(routes)


def norm_kernel(
    blocks, x_ref, gain_ref, gw_ref, routes_ref, gi_ref, slot_ref, table_ref,
    out_ref, gate_ref, low, high, rows_ref, spread,
):
    channels = gain_ref.shape[1]
    low[...] = x_ref[:, :LANES].astype(F32)
    high[...] = x_ref[:, LANES:].astype(F32)
    expert = lax.broadcasted_iota(jnp.int32, (EXPERTS, INNER), 0)

    def step(j, _):
        start = pl.multiple_of(j * INNER, INNER)
        t = jnp.concatenate(
            [
                low[pl.ds(j, channels, stride=blocks), :],
                high[pl.ds(j, channels, stride=blocks), :],
            ],
            1,
        )
        centre = jnp.sum(t, 0, keepdims=True) * (1.0 / channels)
        away = t - centre
        var = jnp.sum(away * away, 0, keepdims=True) * (1.0 / channels)
        scaled = away * lax.rsqrt(var + 1e-05)
        normed = (scaled.T * gain_ref[...]).astype(BF16)
        rows_ref[...] = normed.astype(F32)
        scores = dot_nt(gw_ref[...], normed)
        hot = expert == routes_ref[:, pl.ds(start, INNER)]
        for task in range(TASKS):
            part = scores[task * EXPERTS:(task + 1) * EXPERTS]
            chosen = jnp.sum(jnp.where(hot, part, 0.0), 0, keepdims=True)
            index = gi_ref[task:task + 1, pl.ds(start, INNER)]
            bias = jnp.zeros((1, INNER), F32)
            for entry in range(table_ref.shape[1]):
                bias = jnp.where(index == entry, table_ref[task, entry], bias)
            logit = chosen.astype(BF16).astype(F32) + bias
            gate_ref[task:task + 1, pl.ds(start, INNER)] = jax.nn.sigmoid(logit)

        def move(i, _):
            for u in range(16):
                n = i * 16 + u
                spread[pl.ds(slot_ref[0, start + n], 1), :] = rows_ref[pl.ds(n, 1), :]
            return 0

        lax.fori_loop(0, INNER // 16, move, 0)
        return 0

    lax.fori_loop(0, blocks, step, 0)
    out_ref[...] = spread[...].astype(BF16)


def norm_and_send(x, gain, gate_cols, routes, index, slot, table, slot_total):
    channels = gain.shape[1]
    blocks = x.shape[0] // channels
    tokens = blocks * INNER
    vmem = pl.BlockSpec(memory_space=pltpu.VMEM)
    smem = pl.BlockSpec(memory_space=pltpu.SMEM)
    return pl.pallas_call(
        functools.partial(norm_kernel, blocks),
        in_specs=[vmem] * 5 + [smem] * 2,
        out_specs=[vmem, vmem],
        out_shape=[
            jax.ShapeDtypeStruct((slot_total, channels), BF16),
            jax.ShapeDtypeStruct((8, tokens), F32),
        ],
        scratch_shapes=[
            pltpu.VMEM((x.shape[0], LANES), F32),
            pltpu.VMEM((x.shape[0], LANES), F32),
            pltpu.VMEM((INNER, channels), F32),
            pltpu.VMEM((slot_total, channels), F32),
        ],
        compiler_params=params(),
        name="norm",
    )(x, gain, gate_cols, routes, index, slot, table)


def expert_kernel(x_ref, w_in_ref, w_out_ref, out_ref):
    x = x_ref[...].reshape(-1, x_ref.shape[-1])
    w_in = w_in_ref[...].reshape(-1, w_in_ref.shape[-1])
    w_out = w_out_ref[...].reshape(-1, w_out_ref.shape[-1])
    hidden = jnp.maximum(dot_nt(x, w_in), 0.0).astype(BF16)
    out_ref[...] = dot_nn(hidden, w_out).astype(BF16).reshape(out_ref.shape)


def experts(x, w_in, w_out):
    sources, count, capacity, channels = x.shape
    shares, _, hid, _ = w_in.shape
    x_spec = pl.BlockSpec((sources, 1, capacity, channels), lambda e: (0, e, 0, 0))
    w_spec = pl.BlockSpec((shares, 1, hid, channels), lambda e: (0, e, 0, 0))
    return pl.pallas_call(
        expert_kernel,
        grid=(count,),
        in_specs=[x_spec, w_spec, w_spec],
        out_specs=x_spec,
        out_shape=jax.ShapeDtypeStruct(x.shape, BF16),
        compiler_params=params(),
        name="experts",
    )(x, w_in, w_out)


def finish_kernel(res_ref, gate_ref, slot_ref, out_ref, wide, rows_ref):
    j = pl.program_id(0)

    @pl.when(j == 0)
    def _():
        wide[...] = res_ref[...].astype(F32)

    start = j * INNER

    def move(i, _):
        for u in range(16):
            n = i * 16 + u
            rows_ref[pl.ds(n, 1), :] = wide[pl.ds(slot_ref[0, start + n], 1), :]
        return 0

    lax.fori_loop(0, INNER // 16, move, 0)
    gates = gate_ref[...].T
    rows = rows_ref[...]
    for task in range(TASKS):
        out_ref[task] = (gates[:, task:task + 1] * rows).astype(BF16)


def finish(results, gates, slot):
    slot_total, channels = results.shape
    tokens = gates.shape[1]
    return pl.pallas_call(
        finish_kernel,
        grid=(tokens // INNER,),
        in_specs=[
            pl.BlockSpec((slot_total, channels), lambda j: (0, 0)),
            pl.BlockSpec((8, INNER), lambda j: (0, j)),
            pl.BlockSpec(memory_space=pltpu.SMEM),
        ],
        out_specs=pl.BlockSpec((TASKS, INNER, channels), lambda j: (0, j, 0)),
        out_shape=jax.ShapeDtypeStruct((TASKS, tokens, channels), BF16),
        scratch_shapes=[
            pltpu.VMEM((slot_total, channels), F32),
            pltpu.VMEM((INNER, channels), F32),
        ],
        compiler_params=params(),
        name="finish",
    )(results, gates, slot)


def on_device(
    events, spectral_filter, ln_gain, w_in, w_out, gate_weight, gate_table, routes, gate_index
):
    n_seq = lax.axis_size("seq")
    _, len_dev, user_count, channels = events.shape
    chan_dev = channels // n_seq
    blocks = len_dev // INNER
    capacity = max(2, 2 * len_dev // EXPERTS)
    exp_dev = w_in.shape[0]
    route_row = routes.reshape(1, len_dev)
    index_rows = gate_index.reshape(len_dev, TASKS).T
    gate_cols = gate_weight.transpose(0, 2, 1).reshape(TASKS * EXPERTS, channels)
    all_in = lax.all_gather(w_in, "batch", axis=0, tiled=False)
    all_out = lax.all_gather(w_out, "batch", axis=0, tiled=False)

    turned = turn(events.reshape(len_dev, channels)).reshape(n_seq, chan_dev, blocks, INNER)
    history = lax.all_to_all(turned, "seq", split_axis=0, concat_axis=0, tiled=True)
    slot = slots_of(route_row, capacity)
    if blocks % 16:
        merged = history.transpose(1, 0, 2, 3).reshape(1, chan_dev, n_seq * blocks, INNER)
        summed = spectral(merged, spectral_filter)
        summed = summed.reshape(chan_dev, n_seq, blocks, INNER).transpose(1, 0, 2, 3)
    else:
        summed = spectral(history, spectral_filter)
    returned = lax.all_to_all(summed, "seq", split_axis=0, concat_axis=0, tiled=True)
    outgoing, gates = norm_and_send(
        returned.reshape(channels * blocks, INNER),
        ln_gain.reshape(1, channels),
        gate_cols,
        route_row,
        index_rows,
        slot,
        gate_table,
        EXPERTS * capacity,
    )
    arrived = lax.all_to_all(
        outgoing.reshape(n_seq, exp_dev, capacity, channels),
        "seq", split_axis=0, concat_axis=0, tiled=True,
    )
    done = experts(arrived, all_in, all_out)
    results = lax.all_to_all(done, "seq", split_axis=0, concat_axis=0, tiled=True)
    task_out = finish(results.reshape(EXPERTS * capacity, channels), gates, slot)
    return task_out.reshape(TASKS, 1, len_dev, user_count, channels)


def solution(mesh):
    in_specs = (
        P("batch", "seq", None, None),
        P(None, None, "seq"),
        P(),
        P("seq", "batch", None),
        P("seq", "batch", None),
        P(),
        P(),
        P("batch", "seq", None, None),
        P("batch", "seq", None, None),
    )
    out_specs = P(None, "batch", "seq", None, None)
    return jax.shard_map(
        on_device, mesh=mesh, in_specs=in_specs, out_specs=out_specs, check_vma=False
    )
```

```python
import functools
import math

import jax
import jax.numpy as jnp
import numpy as np
from jax import lax
from jax.experimental import pallas as pl
from jax.experimental.pallas import tpu as pltpu
from jax.sharding import PartitionSpec as P

EXPERTS = 64
TASKS = 3
INNER = 256
LANES = 128
ROWS = 16
VMEM_BYTES = 56 * 2**20
F32 = jnp.float32
BF16 = jnp.bfloat16


def params():
    return pltpu.CompilerParams(vmem_limit_bytes=VMEM_BYTES)


def dot_nt(a, b):
    return lax.dot_general(a, b, (((1,), (1,)), ((), ())), preferred_element_type=F32)


def dot_nn(a, b):
    return jnp.dot(a, b, preferred_element_type=F32)


def tables(length):
    outer = length // INNER

    def angles(rows, cols, points):
        product = np.outer(np.arange(rows), np.arange(cols)) % points
        return product * (2.0 * np.pi / points)

    first = angles(outer, outer, outer)
    inner = angles(INNER, INNER, INNER)
    turn = angles(outer, INNER, length)
    c1, s1, c2, s2 = np.cos(first), np.sin(first), np.cos(inner), np.sin(inner)
    f1 = np.concatenate([c1, -s1], 0)
    m2 = np.block([[c2, s2], [-s2, c2]])
    m3 = np.block([[c2, -s2], [s2, c2]])
    f4 = np.concatenate([c1, -s1], 1) / length
    def bf(a):
        near = a.astype(jnp.bfloat16)
        rest = (a - near.astype(np.float64)).astype(jnp.bfloat16)
        return jnp.asarray(np.stack([near, rest]))

    fl = lambda a: jnp.asarray(a.astype(np.float32))
    return (
        bf(f1), bf(m2), bf(m3), bf(f4),
        fl(np.cos(turn)), fl(np.sin(turn)), fl(np.cos(turn).T), fl(np.sin(turn).T),
    )


def turn_kernel(blocks, parts, x_ref, *refs):
    outs, low, high = refs[:parts], refs[parts], refs[parts + 1]

    def step(j, _):
        rows = x_ref[pl.ds(pl.multiple_of(j * INNER, INNER), INNER), :]
        turned = rows.astype(F32).T
        low[pl.ds(j, LANES, stride=blocks), :] = turned[:, :LANES]
        high[pl.ds(j, LANES, stride=blocks), :] = turned[:, LANES:]
        return 0

    lax.fori_loop(0, blocks, step, 0, unroll=2)
    dests, rows, _ = outs[0].shape
    for part in range(parts):
        for side, half in enumerate((low, high)):
            value = half[...].reshape(dests, parts, rows, LANES)[:, part]
            outs[part][:, :, side * LANES:(side + 1) * LANES] = value.astype(BF16)


def turn(events, chan_dev, parts):
    tokens, channels = events.shape
    blocks = tokens // INNER
    rows = chan_dev // parts * blocks
    dests = LANES // chan_dev
    return pl.pallas_call(
        functools.partial(turn_kernel, blocks, parts),
        grid=(channels // LANES,),
        in_specs=[pl.BlockSpec((tokens, LANES), lambda i: (0, i))],
        out_specs=[pl.BlockSpec((dests, rows, INNER), lambda i: (i, 0, 0))] * parts,
        out_shape=[jax.ShapeDtypeStruct((channels // chan_dev, rows, INNER), BF16)] * parts,
        scratch_shapes=[pltpu.VMEM((LANES * blocks, LANES), F32)] * 2,
        compiler_params=params(),
        name="turn",
    )(events)


def spectral_kernel(
    chans, outer, x_ref, h_ref, f1_ref, m2_ref, m3_ref, f4_ref, tc, ts, tct, tst, out_ref,
    y_ref, g_ref,
):
    x_all = x_ref[...]
    for c in range(chans):
        x = x_all[:, c].reshape(outer, INNER)
        a = dot_nn(f1_ref[0], x) + dot_nn(f1_ref[1], x)
        re, im = a[:outer], a[outer:]
        rows = slice(c * outer, (c + 1) * outer)
        y_ref[rows, :INNER] = (re * tc[...] + im * ts[...]).astype(BF16)
        y_ref[rows, INNER:] = (im * tc[...] - re * ts[...]).astype(BF16)
    y_all = y_ref[...]
    z = dot_nt(m2_ref[0], y_all) + dot_nt(m2_ref[1], y_all)
    for c in range(chans):
        cols = slice(c * outer, (c + 1) * outer)
        zr, zi = z[:INNER, cols], z[INNER:, cols]
        hr, hi = h_ref[0, c], h_ref[1, c]
        g_ref[:INNER, cols] = (zr * hr - zi * hi).astype(BF16)
        g_ref[INNER:, cols] = (zr * hi + zi * hr).astype(BF16)
    g_all = g_ref[...]
    u = dot_nn(m3_ref[0], g_all) + dot_nn(m3_ref[1], g_all)
    for c in range(chans):
        cols = slice(c * outer, (c + 1) * outer)
        ur, ui = u[:INNER, cols], u[INNER:, cols]
        v = jnp.concatenate(
            [
                (ur * tct[...] - ui * tst[...]).astype(BF16),
                (ui * tct[...] + ur * tst[...]).astype(BF16),
            ],
            1,
        )
        y = dot_nt(f4_ref[0], v) + dot_nt(f4_ref[1], v)
        x = x_all[:, c].reshape(outer, INNER)
        total = (x.astype(F32) + y).astype(BF16)
        out_ref[:, c] = total.reshape(out_ref.shape[0], out_ref.shape[2], INNER)


def spectral(x, filt, part):
    parts, chan_dev, blocks, _ = x.shape
    length = parts * blocks * INNER
    outer = length // INNER
    chans = math.gcd(chan_dev, 4)
    consts = tables(length)
    first = part * (chan_dev // chans)
    whole = lambda a: pl.BlockSpec(a.shape, lambda i: (0,) * a.ndim)
    x_spec = pl.BlockSpec((parts, chans, blocks, INNER), lambda i: (0, i, 0, 0))
    return pl.pallas_call(
        functools.partial(spectral_kernel, chans, outer),
        grid=(chan_dev // chans,),
        in_specs=[x_spec, pl.BlockSpec((2, chans, INNER, outer), lambda i: (0, first + i, 0, 0))]
        + [whole(a) for a in consts],
        out_specs=x_spec,
        out_shape=jax.ShapeDtypeStruct(x.shape, BF16),
        scratch_shapes=[
            pltpu.VMEM((chans * outer, 2 * INNER), BF16),
            pltpu.VMEM((2 * INNER, chans * outer), BF16),
        ],
        compiler_params=params(),
        cost_estimate=pl.CostEstimate(
            flops=chan_dev * 2 * 2 * (2 * outer * outer * INNER * 2 + 8 * INNER * INNER * outer),
            bytes_accessed=chan_dev * length * 12,
            transcendentals=0,
        ),
        name="spectral",
    )(x, filt, *consts)


def slot_kernel(exp_dev, reach, routes_ref, slot_ref, size_ref):
    tokens = routes_ref.shape[1]
    row = lax.broadcasted_iota(jnp.int32, (INNER, INNER), 0)
    col = lax.broadcasted_iota(jnp.int32, (INNER, INNER), 1)
    before = (row < col).astype(F32).astype(BF16)
    expert = lax.broadcasted_iota(jnp.int32, (EXPERTS, INNER), 0)

    def hot_of(j):
        return (expert == routes_ref[:, j * INNER:(j + 1) * INNER]).astype(F32)

    count = jnp.zeros((EXPERTS, 1), F32)
    for j in range(tokens // INNER):
        count = count + jnp.sum(hot_of(j), 1, keepdims=True)
    size = jnp.floor((count + (ROWS - 1)) * (1.0 / ROWS)) * ROWS
    wide = jnp.broadcast_to(size, (EXPERTS, LANES))
    size_ref[...] = wide.astype(jnp.int32)
    mine = lax.broadcasted_iota(jnp.int32, (EXPERTS, EXPERTS), 0)
    other = lax.broadcasted_iota(jnp.int32, (EXPERTS, EXPERTS), 1)
    same = lax.div(mine, exp_dev) == lax.div(other, exp_dev)
    earlier = jnp.where(same & (other < mine), 1.0, 0.0).astype(BF16)
    offset = dot_nn(earlier, wide.astype(BF16))[:, :1]
    owner = lax.div(lax.broadcasted_iota(jnp.int32, (EXPERTS, 1), 0), exp_dev)
    base = offset + (owner * reach).astype(F32)
    for j in range(tokens // INNER):
        hot = hot_of(j)
        rank = dot_nn(hot.astype(BF16), before)
        value = jnp.sum(hot * (rank + base), 0, keepdims=True)
        slot_ref[:, j * INNER:(j + 1) * INNER] = value.astype(jnp.int32)
        base = base + jnp.sum(hot, 1, keepdims=True)


def slots_of(routes, exp_dev, reach):
    return pl.pallas_call(
        functools.partial(slot_kernel, exp_dev, reach),
        out_shape=[
            jax.ShapeDtypeStruct(routes.shape, jnp.int32),
            jax.ShapeDtypeStruct((EXPERTS, LANES), jnp.int32),
        ],
        compiler_params=params(),
        name="slots",
    )(routes)


def norm_kernel(
    blocks, parts, chunks, *refs
):
    x_refs, refs = refs[:parts], refs[parts:]
    gain_ref, gw_ref, routes_ref, gi_ref, slot_ref, table_ref, *refs = refs
    out_refs, refs = refs[:chunks], refs[chunks:]
    gate_ref, low, high, rows_ref, spread = refs
    channels = gain_ref.shape[1]
    sources, rows, _ = x_refs[0].shape
    for source in range(sources):
        for part in range(parts):
            x = x_refs[part][source].astype(F32)
            at = pl.ds((source * parts + part) * rows, rows)
            low[at, :] = x[:, :LANES]
            high[at, :] = x[:, LANES:]
    expert = lax.broadcasted_iota(jnp.int32, (EXPERTS, INNER), 0)

    def step(j, _):
        start = pl.multiple_of(j * INNER, INNER)
        t = jnp.concatenate(
            [
                low[pl.ds(j, channels, stride=blocks), :],
                high[pl.ds(j, channels, stride=blocks), :],
            ],
            1,
        )
        centre = jnp.sum(t, 0, keepdims=True) * (1.0 / channels)
        away = t - centre
        var = jnp.sum(away * away, 0, keepdims=True) * (1.0 / channels)
        scaled = away * lax.rsqrt(var + 1e-05)
        normed = (scaled.T * gain_ref[...]).astype(BF16)
        rows_ref[...] = normed.astype(F32)
        scores = dot_nt(gw_ref[...], normed)
        hot = expert == routes_ref[:, pl.ds(start, INNER)]
        for task in range(TASKS):
            part = scores[task * EXPERTS:(task + 1) * EXPERTS]
            chosen = jnp.sum(jnp.where(hot, part, 0.0), 0, keepdims=True)
            index = gi_ref[task:task + 1, pl.ds(start, INNER)]
            bias = jnp.zeros((1, INNER), F32)
            for entry in range(table_ref.shape[1]):
                bias = jnp.where(index == entry, table_ref[task, entry], bias)
            logit = chosen.astype(BF16).astype(F32) + bias
            gate_ref[task:task + 1, pl.ds(start, INNER)] = jax.nn.sigmoid(logit)

        def move(i, _):
            for u in range(16):
                n = i * 16 + u
                spread[pl.ds(slot_ref[0, start + n], 1), :] = rows_ref[pl.ds(n, 1), :]
            return 0

        lax.fori_loop(0, INNER // 16, move, 0)
        return 0

    lax.fori_loop(0, blocks, step, 0)
    size = spread.shape[0] // chunks
    for chunk in range(chunks):
        out_refs[chunk][...] = spread[chunk * size:(chunk + 1) * size, :].astype(BF16)


def norm_and_send(xs, gain, gate_cols, routes, index, slot, table, slot_total, chunks):
    channels = gain.shape[1]
    parts = len(xs)
    tokens = routes.shape[1]
    blocks = tokens // INNER
    vmem = pl.BlockSpec(memory_space=pltpu.VMEM)
    smem = pl.BlockSpec(memory_space=pltpu.SMEM)
    return pl.pallas_call(
        functools.partial(norm_kernel, blocks, parts, chunks),
        in_specs=[vmem] * (parts + 4) + [smem] * 2,
        out_specs=[vmem] * (chunks + 1),
        out_shape=[jax.ShapeDtypeStruct((slot_total // chunks, channels), BF16)] * chunks
        + [jax.ShapeDtypeStruct((8, tokens), F32)],
        scratch_shapes=[
            pltpu.VMEM((channels * blocks, LANES), F32),
            pltpu.VMEM((channels * blocks, LANES), F32),
            pltpu.VMEM((INNER, channels), F32),
            pltpu.VMEM((slot_total, channels), F32),
        ],
        compiler_params=params(),
        name="norm",
    )(*xs, gain, gate_cols, routes, index, slot, table)


def expert_kernel(chunk, x_ref, w_in_ref, w_out_ref, start_ref, size_ref, out_ref, held, made):
    e = pl.program_id(0)
    sources, height, channels = x_ref.shape

    def piece(source):
        start = start_ref[source, e] - chunk * height
        low = jnp.clip(start, 0, height)
        high = jnp.clip(start + size_ref[source, e], 0, height)
        return low, lax.div(high - low, ROWS)

    def at(first, i):
        return pl.ds(pl.multiple_of(first + i * ROWS, ROWS), ROWS)

    def fetch(source, filled):
        low, count = piece(source)

        def one(i, _):
            held[at(filled, i), :] = x_ref[source, at(low, i), :]
            return 0

        lax.fori_loop(0, count, one, 0)
        return filled + count * ROWS

    total = lax.fori_loop(0, sources, fetch, 0)
    w_in = w_in_ref[...].reshape(-1, channels)
    w_out = w_out_ref[...].reshape(-1, channels)

    def tile(t, _):
        rows = pl.ds(pl.multiple_of(t * INNER, INNER), INNER)
        hidden = jnp.maximum(dot_nt(held[rows, :], w_in), 0.0).astype(BF16)
        made[rows, :] = dot_nn(hidden, w_out).astype(BF16)
        return 0

    lax.fori_loop(0, lax.div(total + INNER - 1, INNER), tile, 0)

    def give(source, filled):
        low, count = piece(source)

        def one(i, _):
            out_ref[source, at(low, i), :] = made[at(filled, i), :]
            return 0

        lax.fori_loop(0, count, one, 0)
        return filled + count * ROWS

    lax.fori_loop(0, sources, give, 0)


def experts(x, w_in, w_out, start, size, chunk, chunks, capacity):
    sources, height, channels = x.shape
    shares, count, hid, _ = w_in.shape
    most = -(-sources * capacity // INNER) * INNER
    x_spec = pl.BlockSpec(x.shape, lambda e: (0, 0, 0))
    w_spec = pl.BlockSpec((shares, 1, hid, channels), lambda e: (0, e, 0, 0))
    smem = pl.BlockSpec(memory_space=pltpu.SMEM)
    return pl.pallas_call(
        functools.partial(expert_kernel, chunk),
        grid=(count,),
        in_specs=[x_spec, w_spec, w_spec, smem, smem],
        out_specs=x_spec,
        out_shape=jax.ShapeDtypeStruct(x.shape, BF16),
        scratch_shapes=[pltpu.VMEM((most, channels), BF16)] * 2,
        compiler_params=params(),
        cost_estimate=pl.CostEstimate(
            flops=4 * sources * height * channels * shares * hid,
            bytes_accessed=2 * (2 * x.size + w_in.size + w_out.size),
            transcendentals=0,
        ),
        name="experts",
    )(x, w_in, w_out, start, size)


def finish_kernel(chunks, *refs):
    res_refs, refs = refs[:chunks], refs[chunks:]
    gate_ref, slot_ref, out_ref, wide, rows_ref = refs
    j = pl.program_id(0)

    @pl.when(j == 0)
    def _():
        size = res_refs[0].shape[0]
        for chunk in range(chunks):
            wide[chunk * size:(chunk + 1) * size, :] = res_refs[chunk][...].astype(F32)

    start = j * INNER

    def move(i, _):
        for u in range(16):
            n = i * 16 + u
            rows_ref[pl.ds(n, 1), :] = wide[pl.ds(slot_ref[0, start + n], 1), :]
        return 0

    lax.fori_loop(0, INNER // 16, move, 0)
    gates = gate_ref[...].T
    rows = rows_ref[...]
    for task in range(TASKS):
        out_ref[task] = (gates[:, task:task + 1] * rows).astype(BF16)


def finish(results, gates, slot):
    chunks = len(results)
    size, channels = results[0].shape
    tokens = gates.shape[1]
    return pl.pallas_call(
        functools.partial(finish_kernel, chunks),
        grid=(tokens // INNER,),
        in_specs=[pl.BlockSpec((size, channels), lambda j: (0, 0))] * chunks
        + [
            pl.BlockSpec((8, INNER), lambda j: (0, j)),
            pl.BlockSpec(memory_space=pltpu.SMEM),
        ],
        out_specs=pl.BlockSpec((TASKS, INNER, channels), lambda j: (0, j, 0)),
        out_shape=jax.ShapeDtypeStruct((TASKS, tokens, channels), BF16),
        scratch_shapes=[
            pltpu.VMEM((chunks * size, channels), F32),
            pltpu.VMEM((INNER, channels), F32),
        ],
        compiler_params=params(),
        name="finish",
    )(*results, gates, slot)


def on_device(
    events, spectral_filter, ln_gain, w_in, w_out, gate_weight, gate_table, routes, gate_index
):
    n_seq = lax.axis_size("seq")
    _, len_dev, user_count, channels = events.shape
    chan_dev = channels // n_seq
    blocks = len_dev // INNER
    capacity = max(2, 2 * len_dev // EXPERTS)
    exp_dev = w_in.shape[0]
    reach = exp_dev * capacity
    parts = 2 if chan_dev % 16 == 0 and blocks % 16 == 0 else 1
    route_row = routes.reshape(1, len_dev)
    index_rows = gate_index.reshape(len_dev, TASKS).T
    gate_cols = gate_weight.transpose(0, 2, 1).reshape(TASKS * EXPERTS, channels)

    slot, size = slots_of(route_row, exp_dev, reach)
    sizes = lax.all_gather(size[:, 0], ("batch", "seq"), axis=0, tiled=False)
    heights = tier_heights(reach)
    tallest = jnp.max(jnp.sum(sizes.reshape(-1, n_seq, exp_dev), -1))
    tier = sum((tallest > height).astype(jnp.int32) for height in heights[:-1])
    own = lax.dynamic_slice(
        sizes,
        (lax.axis_index("batch") * n_seq, lax.axis_index("seq") * exp_dev),
        (n_seq, exp_dev),
    )
    ahead = jnp.arange(exp_dev)[:, None] > jnp.arange(exp_dev)[None, :]
    start = jnp.sum(jnp.where(ahead[None], own[:, None, :], 0), -1)
    all_in = lax.all_gather(w_in, "batch", axis=0, tiled=False)
    all_out = lax.all_gather(w_out, "batch", axis=0, tiled=False)

    length = len_dev * n_seq
    filt = spectral_filter.transpose(0, 2, 1).reshape(2, chan_dev, INNER, length // INNER)
    chan_part = chan_dev // parts
    returned = []
    for part, turned in enumerate(turn(events.reshape(len_dev, channels), chan_dev, parts)):
        history = lax.all_to_all(turned, "seq", split_axis=0, concat_axis=0, tiled=True)
        history = history.reshape(n_seq, chan_part, blocks, INNER)
        if blocks % 16:
            merged = history.transpose(1, 0, 2, 3).reshape(1, chan_part, n_seq * blocks, INNER)
            summed = spectral(merged, filt, part)
            summed = summed.reshape(chan_part, n_seq, blocks, INNER).transpose(1, 0, 2, 3)
        else:
            summed = spectral(history, filt, part)
        summed = summed.reshape(n_seq, chan_part * blocks, INNER)
        returned.append(
            lax.all_to_all(summed, "seq", split_axis=0, concat_axis=0, tiled=True)
        )

    def mixture(height, returned, slot, start, own, all_in, all_out):
        chunks = 2 if height % (2 * ROWS) == 0 else 1
        chunk_rows = height // chunks
        owner, local = slot // reach, slot % reach
        chunk_of = local // chunk_rows
        place = (chunk_of * n_seq + owner) * chunk_rows + local % chunk_rows
        *outgoing, gates = norm_and_send(
            returned,
            ln_gain.reshape(1, channels),
            gate_cols,
            route_row,
            index_rows,
            place,
            gate_table,
            n_seq * height,
            chunks,
        )
        results = []
        for chunk, rows in enumerate(outgoing):
            arrived = lax.all_to_all(
                rows.reshape(n_seq, chunk_rows, channels),
                "seq", split_axis=0, concat_axis=0, tiled=True,
            )
            done = experts(arrived, all_in, all_out, start, own, chunk, chunks, capacity)
            back = lax.all_to_all(done, "seq", split_axis=0, concat_axis=0, tiled=True)
            results.append(back.reshape(n_seq * chunk_rows, channels))
        return finish(results, gates, place)

    branches = [functools.partial(mixture, height) for height in heights]
    task_out = lax.switch(tier, branches, returned, slot, start, own, all_in, all_out)
    return task_out.reshape(TASKS, 1, len_dev, user_count, channels)


def tier_heights(reach):
    if reach % 1024:
        return [reach]
    return [reach // 32 * share for share in (22, 23, 24, 26, 28, 32)]


def solution(mesh):
    in_specs = (
        P("batch", "seq", None, None),
        P(None, None, "seq"),
        P(),
        P("seq", "batch", None),
        P("seq", "batch", None),
        P(),
        P(),
        P("batch", "seq", None, None),
        P("batch", "seq", None, None),
    )
    out_specs = P(None, "batch", "seq", None, None)
    return jax.shard_map(
        on_device, mesh=mesh, in_specs=in_specs, out_specs=out_specs, check_vma=False
    )
```

```python
import functools
import math

import jax
import jax.numpy as jnp
import numpy as np
from jax import lax
from jax.experimental import pallas as pl
from jax.experimental.pallas import tpu as pltpu
from jax.sharding import PartitionSpec as P

EXPERTS = 64
TASKS = 3
INNER = 256
LANES = 128
ROWS = 16
VMEM_BYTES = 56 * 2**20
F32 = jnp.float32
BF16 = jnp.bfloat16


def params():
    return pltpu.CompilerParams(vmem_limit_bytes=VMEM_BYTES)


def dot_nt(a, b):
    return lax.dot_general(a, b, (((1,), (1,)), ((), ())), preferred_element_type=F32)


def dot_nn(a, b):
    return jnp.dot(a, b, preferred_element_type=F32)


def tables(length):
    outer = length // INNER

    def angles(rows, cols, points):
        product = np.outer(np.arange(rows), np.arange(cols)) % points
        return product * (2.0 * np.pi / points)

    first = angles(outer, outer, outer)
    inner = angles(INNER, INNER, INNER)
    turn = angles(outer, INNER, length)
    c1, s1, c2, s2 = np.cos(first), np.sin(first), np.cos(inner), np.sin(inner)
    f1 = np.concatenate([c1, -s1], 0)
    m2 = np.block([[c2, s2], [-s2, c2]])
    m3 = np.block([[c2, -s2], [s2, c2]])
    f4 = np.concatenate([c1, -s1], 1) / length
    def bf(a):
        near = a.astype(jnp.bfloat16)
        rest = (a - near.astype(np.float64)).astype(jnp.bfloat16)
        return jnp.asarray(np.stack([near, rest]))

    fl = lambda a: jnp.asarray(a.astype(np.float32))
    return (
        bf(f1), bf(m2), bf(m3), bf(f4),
        fl(np.cos(turn)), fl(np.sin(turn)), fl(np.cos(turn).T), fl(np.sin(turn).T),
    )


def turn_kernel(blocks, parts, x_ref, *refs):
    outs, low, high = refs[:parts], refs[parts], refs[parts + 1]

    def step(j, _):
        rows = x_ref[pl.ds(pl.multiple_of(j * INNER, INNER), INNER), :]
        turned = rows.astype(F32).T
        low[pl.ds(j, LANES, stride=blocks), :] = turned[:, :LANES]
        high[pl.ds(j, LANES, stride=blocks), :] = turned[:, LANES:]
        return 0

    lax.fori_loop(0, blocks, step, 0, unroll=2)
    dests, rows, _ = outs[0].shape
    for part in range(parts):
        for side, half in enumerate((low, high)):
            value = half[...].reshape(dests, parts, rows, LANES)[:, part]
            outs[part][:, :, side * LANES:(side + 1) * LANES] = value.astype(BF16)


def turn(events, chan_dev, parts):
    tokens, channels = events.shape
    blocks = tokens // INNER
    rows = chan_dev // parts * blocks
    dests = LANES // chan_dev
    return pl.pallas_call(
        functools.partial(turn_kernel, blocks, parts),
        grid=(channels // LANES,),
        in_specs=[pl.BlockSpec((tokens, LANES), lambda i: (0, i))],
        out_specs=[pl.BlockSpec((dests, rows, INNER), lambda i: (i, 0, 0))] * parts,
        out_shape=[jax.ShapeDtypeStruct((channels // chan_dev, rows, INNER), BF16)] * parts,
        scratch_shapes=[pltpu.VMEM((LANES * blocks, LANES), F32)] * 2,
        compiler_params=params(),
        name="turn",
    )(events)


def spectral_kernel(
    chans, outer, x_ref, h_ref, f1_ref, m2_ref, m3_ref, f4_ref, tc, ts, tct, tst, out_ref,
    y_ref, g_ref,
):
    x_all = x_ref[...]
    for c in range(chans):
        x = x_all[:, c].reshape(outer, INNER)
        a = dot_nn(f1_ref[0], x) + dot_nn(f1_ref[1], x)
        re, im = a[:outer], a[outer:]
        rows = slice(c * outer, (c + 1) * outer)
        y_ref[rows, :INNER] = (re * tc[...] + im * ts[...]).astype(BF16)
        y_ref[rows, INNER:] = (im * tc[...] - re * ts[...]).astype(BF16)
    y_all = y_ref[...]
    z = dot_nt(m2_ref[0], y_all) + dot_nt(m2_ref[1], y_all)
    for c in range(chans):
        cols = slice(c * outer, (c + 1) * outer)
        zr, zi = z[:INNER, cols], z[INNER:, cols]
        hr, hi = h_ref[0, c], h_ref[1, c]
        g_ref[:INNER, cols] = (zr * hr - zi * hi).astype(BF16)
        g_ref[INNER:, cols] = (zr * hi + zi * hr).astype(BF16)
    g_all = g_ref[...]
    u = dot_nn(m3_ref[0], g_all) + dot_nn(m3_ref[1], g_all)
    for c in range(chans):
        cols = slice(c * outer, (c + 1) * outer)
        ur, ui = u[:INNER, cols], u[INNER:, cols]
        v = jnp.concatenate(
            [
                (ur * tct[...] - ui * tst[...]).astype(BF16),
                (ui * tct[...] + ur * tst[...]).astype(BF16),
            ],
            1,
        )
        y = dot_nt(f4_ref[0], v) + dot_nt(f4_ref[1], v)
        x = x_all[:, c].reshape(outer, INNER)
        total = (x.astype(F32) + y).astype(BF16)
        out_ref[:, c] = total.reshape(out_ref.shape[0], out_ref.shape[2], INNER)


def spectral(x, filt, part):
    parts, chan_dev, blocks, _ = x.shape
    length = parts * blocks * INNER
    outer = length // INNER
    chans = math.gcd(chan_dev, 4)
    consts = tables(length)
    first = part * (chan_dev // chans)
    whole = lambda a: pl.BlockSpec(a.shape, lambda i: (0,) * a.ndim)
    x_spec = pl.BlockSpec((parts, chans, blocks, INNER), lambda i: (0, i, 0, 0))
    return pl.pallas_call(
        functools.partial(spectral_kernel, chans, outer),
        grid=(chan_dev // chans,),
        in_specs=[x_spec, pl.BlockSpec((2, chans, INNER, outer), lambda i: (0, first + i, 0, 0))]
        + [whole(a) for a in consts],
        out_specs=x_spec,
        out_shape=jax.ShapeDtypeStruct(x.shape, BF16),
        scratch_shapes=[
            pltpu.VMEM((chans * outer, 2 * INNER), BF16),
            pltpu.VMEM((2 * INNER, chans * outer), BF16),
        ],
        compiler_params=params(),
        cost_estimate=pl.CostEstimate(
            flops=chan_dev * 2 * 2 * (2 * outer * outer * INNER * 2 + 8 * INNER * INNER * outer),
            bytes_accessed=chan_dev * length * 12,
            transcendentals=0,
        ),
        name="spectral",
    )(x, filt, *consts)


def slot_kernel(exp_dev, reach, routes_ref, slot_ref, size_ref):
    tokens = routes_ref.shape[1]
    row = lax.broadcasted_iota(jnp.int32, (INNER, INNER), 0)
    col = lax.broadcasted_iota(jnp.int32, (INNER, INNER), 1)
    before = (row < col).astype(F32).astype(BF16)
    expert = lax.broadcasted_iota(jnp.int32, (EXPERTS, INNER), 0)

    def hot_of(j):
        return (expert == routes_ref[:, j * INNER:(j + 1) * INNER]).astype(F32)

    count = jnp.zeros((EXPERTS, 1), F32)
    for j in range(tokens // INNER):
        count = count + jnp.sum(hot_of(j), 1, keepdims=True)
    wide = jnp.broadcast_to(count, (EXPERTS, LANES))
    lanes = jnp.concatenate([wide, jnp.zeros((LANES - EXPERTS, LANES), F32)], 0).T
    size_ref[...] = lanes[:size_ref.shape[0]].astype(jnp.int32)
    mine = lax.broadcasted_iota(jnp.int32, (EXPERTS, EXPERTS), 0)
    other = lax.broadcasted_iota(jnp.int32, (EXPERTS, EXPERTS), 1)
    same = lax.div(mine, exp_dev) == lax.div(other, exp_dev)
    earlier = jnp.where(same & (other < mine), 1.0, 0.0).astype(BF16)
    offset = dot_nn(earlier, wide.astype(BF16))[:, :1]
    owner = lax.div(lax.broadcasted_iota(jnp.int32, (EXPERTS, 1), 0), exp_dev)
    base = offset + (owner * reach).astype(F32)
    for j in range(tokens // INNER):
        hot = hot_of(j)
        rank = dot_nn(hot.astype(BF16), before)
        value = jnp.sum(hot * (rank + base), 0, keepdims=True)
        slot_ref[:, j * INNER:(j + 1) * INNER] = value.astype(jnp.int32)
        base = base + jnp.sum(hot, 1, keepdims=True)


def slots_of(routes, exp_dev, reach):
    return pl.pallas_call(
        functools.partial(slot_kernel, exp_dev, reach),
        out_shape=[
            jax.ShapeDtypeStruct(routes.shape, jnp.int32),
            jax.ShapeDtypeStruct((8, LANES), jnp.int32),
        ],
        compiler_params=params(),
        name="slots",
    )(routes)


def norm_kernel(
    blocks, parts, chunks, *refs
):
    x_refs, refs = refs[:parts], refs[parts:]
    gain_ref, gw_ref, routes_ref, gi_ref, slot_ref, table_ref, *refs = refs
    out_refs, refs = refs[:chunks], refs[chunks:]
    gate_ref, low, high, rows_ref, spread = refs
    channels = gain_ref.shape[1]
    sources, rows, _ = x_refs[0].shape
    for source in range(sources):
        for part in range(parts):
            x = x_refs[part][source].astype(F32)
            at = pl.ds((source * parts + part) * rows, rows)
            low[at, :] = x[:, :LANES]
            high[at, :] = x[:, LANES:]
    expert = lax.broadcasted_iota(jnp.int32, (EXPERTS, INNER), 0)

    def step(j, _):
        start = pl.multiple_of(j * INNER, INNER)
        t = jnp.concatenate(
            [
                low[pl.ds(j, channels, stride=blocks), :],
                high[pl.ds(j, channels, stride=blocks), :],
            ],
            1,
        )
        centre = jnp.sum(t, 0, keepdims=True) * (1.0 / channels)
        away = t - centre
        var = jnp.sum(away * away, 0, keepdims=True) * (1.0 / channels)
        scaled = away * lax.rsqrt(var + 1e-05)
        normed = (scaled.T * gain_ref[...]).astype(BF16)
        rows_ref[...] = normed.astype(F32)
        scores = dot_nt(gw_ref[...], normed)
        hot = expert == routes_ref[:, pl.ds(start, INNER)]
        for task in range(TASKS):
            part = scores[task * EXPERTS:(task + 1) * EXPERTS]
            chosen = jnp.sum(jnp.where(hot, part, 0.0), 0, keepdims=True)
            index = gi_ref[task:task + 1, pl.ds(start, INNER)]
            bias = jnp.zeros((1, INNER), F32)
            for entry in range(table_ref.shape[1]):
                bias = jnp.where(index == entry, table_ref[task, entry], bias)
            logit = chosen.astype(BF16).astype(F32) + bias
            gate_ref[task:task + 1, pl.ds(start, INNER)] = jax.nn.sigmoid(logit)

        def move(i, _):
            first = pl.multiple_of(i * 16, 16)
            places = [slot_ref[0, start + first + u] for u in range(16)]
            rows = rows_ref[pl.ds(first, 16), :]
            for u in range(16):
                spread[pl.ds(places[u], 1), :] = rows[u:u + 1, :]
            return 0

        lax.fori_loop(0, INNER // 16, move, 0)
        return 0

    lax.fori_loop(0, blocks, step, 0)
    size = spread.shape[0] // chunks
    for chunk in range(chunks):
        out_refs[chunk][...] = spread[chunk * size:(chunk + 1) * size, :].astype(BF16)


def norm_and_send(xs, gain, gate_cols, routes, index, slot, table, slot_total, chunks):
    channels = gain.shape[1]
    parts = len(xs)
    tokens = routes.shape[1]
    blocks = tokens // INNER
    vmem = pl.BlockSpec(memory_space=pltpu.VMEM)
    smem = pl.BlockSpec(memory_space=pltpu.SMEM)
    return pl.pallas_call(
        functools.partial(norm_kernel, blocks, parts, chunks),
        in_specs=[vmem] * (parts + 4) + [smem] * 2,
        out_specs=[vmem] * (chunks + 1),
        out_shape=[jax.ShapeDtypeStruct((slot_total // chunks, channels), BF16)] * chunks
        + [jax.ShapeDtypeStruct((8, tokens), F32)],
        scratch_shapes=[
            pltpu.VMEM((channels * blocks, LANES), F32),
            pltpu.VMEM((channels * blocks, LANES), F32),
            pltpu.VMEM((INNER, channels), F32),
            pltpu.VMEM((slot_total, channels), F32),
        ],
        compiler_params=params(),
        name="norm",
    )(*xs, gain, gate_cols, routes, index, slot, table)


def expert_kernel(chunk, x_ref, w_in_ref, w_out_ref, start_ref, size_ref, out_ref, held, made):
    e = pl.program_id(0)
    sources, height, channels = x_ref.shape

    def piece(source):
        start = start_ref[source, e] - chunk * height
        low = jnp.clip(start, 0, height)
        high = jnp.clip(start + size_ref[source, e], 0, height)
        first = lax.div(low, ROWS)
        count = jnp.where(high > low, lax.div(high + (ROWS - 1), ROWS) - first, 0)
        return low, high, first * ROWS, count

    def at(first, i):
        return pl.ds(pl.multiple_of(first + i * ROWS, ROWS), ROWS)

    def fetch(source, filled):
        _, _, first, count = piece(source)

        def one(i, _):
            held[at(filled, i), :] = x_ref[source, at(first, i), :]
            return 0

        lax.fori_loop(0, count, one, 0)
        return filled + count * ROWS

    total = lax.fori_loop(0, sources, fetch, 0)
    w_in = w_in_ref[...].reshape(-1, channels)
    w_out = w_out_ref[...].reshape(-1, channels)

    def tile(t, _):
        rows = pl.ds(pl.multiple_of(t * INNER, INNER), INNER)
        hidden = jnp.maximum(dot_nt(held[rows, :], w_in), 0.0).astype(BF16)
        made[rows, :] = dot_nn(hidden, w_out).astype(BF16)
        return 0

    lax.fori_loop(0, lax.div(total + INNER - 1, INNER), tile, 0)

    offset = lax.broadcasted_iota(jnp.int32, (ROWS, channels), 0)

    def give(source, filled):
        low, high, first, count = piece(source)

        def one(i, _):
            row = offset + (first + i * ROWS)
            new = made[at(filled, i), :].astype(F32)
            old = out_ref[source, at(first, i), :].astype(F32)
            mine = (row >= low) & (row < high)
            out_ref[source, at(first, i), :] = jnp.where(mine, new, old).astype(BF16)
            return 0

        lax.fori_loop(0, count, one, 0)
        return filled + count * ROWS

    lax.fori_loop(0, sources, give, 0)


def experts(x, w_in, w_out, start, size, chunk, chunks, capacity):
    sources, height, channels = x.shape
    shares, count, hid, _ = w_in.shape
    most = -(-sources * (capacity + 2 * ROWS) // INNER) * INNER
    x_spec = pl.BlockSpec(x.shape, lambda e: (0, 0, 0))
    w_spec = pl.BlockSpec((shares, 1, hid, channels), lambda e: (0, e, 0, 0))
    smem = pl.BlockSpec(memory_space=pltpu.SMEM)
    return pl.pallas_call(
        functools.partial(expert_kernel, chunk),
        grid=(count,),
        in_specs=[x_spec, w_spec, w_spec, smem, smem],
        out_specs=x_spec,
        out_shape=jax.ShapeDtypeStruct(x.shape, BF16),
        scratch_shapes=[pltpu.VMEM((most, channels), BF16)] * 2,
        compiler_params=params(),
        cost_estimate=pl.CostEstimate(
            flops=4 * sources * height * channels * shares * hid,
            bytes_accessed=2 * (2 * x.size + w_in.size + w_out.size),
            transcendentals=0,
        ),
        name="experts",
    )(x, w_in, w_out, start, size)


def finish_kernel(chunks, *refs):
    res_refs, refs = refs[:chunks], refs[chunks:]
    gate_ref, slot_ref, out_ref, wide, rows_ref = refs
    j = pl.program_id(0)

    @pl.when(j == 0)
    def _():
        size = res_refs[0].shape[0]
        for chunk in range(chunks):
            wide[chunk * size:(chunk + 1) * size, :] = res_refs[chunk][...].astype(F32)

    start = j * INNER

    def move(i, _):
        first = pl.multiple_of(i * 16, 16)
        rows = [wide[pl.ds(slot_ref[0, start + first + u], 1), :] for u in range(16)]
        for u in range(16):
            rows_ref[pl.ds(first + u, 1), :] = rows[u]
        return 0

    lax.fori_loop(0, INNER // 16, move, 0)
    gates = gate_ref[...].T
    rows = rows_ref[...]
    for task in range(TASKS):
        out_ref[task] = (gates[:, task:task + 1] * rows).astype(BF16)


def finish(results, gates, slot):
    chunks = len(results)
    size, channels = results[0].shape
    tokens = gates.shape[1]
    return pl.pallas_call(
        functools.partial(finish_kernel, chunks),
        grid=(tokens // INNER,),
        in_specs=[pl.BlockSpec((size, channels), lambda j: (0, 0))] * chunks
        + [
            pl.BlockSpec((8, INNER), lambda j: (0, j)),
            pl.BlockSpec(memory_space=pltpu.SMEM),
        ],
        out_specs=pl.BlockSpec((TASKS, INNER, channels), lambda j: (0, j, 0)),
        out_shape=jax.ShapeDtypeStruct((TASKS, tokens, channels), BF16),
        scratch_shapes=[
            pltpu.VMEM((chunks * size, channels), F32),
            pltpu.VMEM((INNER, channels), F32),
        ],
        compiler_params=params(),
        name="finish",
    )(*results, gates, slot)


def on_device(
    events, spectral_filter, ln_gain, w_in, w_out, gate_weight, gate_table, routes, gate_index
):
    n_seq = lax.axis_size("seq")
    _, len_dev, user_count, channels = events.shape
    chan_dev = channels // n_seq
    blocks = len_dev // INNER
    capacity = max(2, 2 * len_dev // EXPERTS)
    exp_dev = w_in.shape[0]
    reach = exp_dev * capacity
    parts = 2 if chan_dev % 16 == 0 and blocks % 16 == 0 else 1
    route_row = routes.reshape(1, len_dev)
    index_rows = gate_index.reshape(len_dev, TASKS).T
    gate_cols = gate_weight.transpose(0, 2, 1).reshape(TASKS * EXPERTS, channels)

    slot, size = slots_of(route_row, exp_dev, reach)
    sizes = lax.all_gather(size, ("batch", "seq"), axis=0, tiled=True)[::8, :EXPERTS]
    events, _ = lax.optimization_barrier((events, size))
    heights = tier_heights(reach)
    tallest = jnp.max(jnp.sum(sizes.reshape(-1, n_seq, exp_dev), -1))
    tier = sum((tallest > height).astype(jnp.int32) for height in heights[:-1])
    own = lax.dynamic_slice(
        sizes,
        (lax.axis_index("batch") * n_seq, lax.axis_index("seq") * exp_dev),
        (n_seq, exp_dev),
    )
    ahead = jnp.arange(exp_dev)[:, None] > jnp.arange(exp_dev)[None, :]
    start = jnp.sum(jnp.where(ahead[None], own[:, None, :], 0), -1)
    all_in = lax.all_gather(w_in, "batch", axis=0, tiled=False)
    all_out = lax.all_gather(w_out, "batch", axis=0, tiled=False)

    length = len_dev * n_seq
    filt = spectral_filter.transpose(0, 2, 1).reshape(2, chan_dev, INNER, length // INNER)
    chan_part = chan_dev // parts
    returned = []
    for part, turned in enumerate(turn(events.reshape(len_dev, channels), chan_dev, parts)):
        history = lax.all_to_all(turned, "seq", split_axis=0, concat_axis=0, tiled=True)
        history = history.reshape(n_seq, chan_part, blocks, INNER)
        if blocks % 16:
            merged = history.transpose(1, 0, 2, 3).reshape(1, chan_part, n_seq * blocks, INNER)
            summed = spectral(merged, filt, part)
            summed = summed.reshape(chan_part, n_seq, blocks, INNER).transpose(1, 0, 2, 3)
        else:
            summed = spectral(history, filt, part)
        summed = summed.reshape(n_seq, chan_part * blocks, INNER)
        returned.append(
            lax.all_to_all(summed, "seq", split_axis=0, concat_axis=0, tiled=True)
        )

    def mixture(height, returned, slot, start, own, all_in, all_out):
        chunks = 2 if height % (2 * ROWS) == 0 else 1
        chunk_rows = height // chunks
        owner, local = slot // reach, slot % reach
        chunk_of = local // chunk_rows
        place = (chunk_of * n_seq + owner) * chunk_rows + local % chunk_rows
        *outgoing, gates = norm_and_send(
            returned,
            ln_gain.reshape(1, channels),
            gate_cols,
            route_row,
            index_rows,
            place,
            gate_table,
            n_seq * height,
            chunks,
        )
        results = []
        for chunk, rows in enumerate(outgoing):
            arrived = lax.all_to_all(
                rows.reshape(n_seq, chunk_rows, channels),
                "seq", split_axis=0, concat_axis=0, tiled=True,
            )
            done = experts(arrived, all_in, all_out, start, own, chunk, chunks, capacity)
            back = lax.all_to_all(done, "seq", split_axis=0, concat_axis=0, tiled=True)
            results.append(back.reshape(n_seq * chunk_rows, channels))
        return finish(results, gates, place)

    branches = [functools.partial(mixture, height) for height in heights]
    task_out = lax.switch(tier, branches, returned, slot, start, own, all_in, all_out)
    return task_out.reshape(TASKS, 1, len_dev, user_count, channels)


def tier_heights(reach):
    if reach % 1024:
        return [reach]
    return [reach // 32 * share for share in (21, 22, 23, 24, 25, 26, 28, 32)]


def solution(mesh):
    in_specs = (
        P("batch", "seq", None, None),
        P(None, None, "seq"),
        P(),
        P("seq", "batch", None),
        P("seq", "batch", None),
        P(),
        P(),
        P("batch", "seq", None, None),
        P("batch", "seq", None, None),
    )
    out_specs = P(None, "batch", "seq", None, None)
    return jax.shard_map(
        on_device, mesh=mesh, in_specs=in_specs, out_specs=out_specs, check_vma=False
    )
```

```python
import functools
import math

import jax
import jax.numpy as jnp
import numpy as np
from jax import lax
from jax.experimental import pallas as pl
from jax.experimental.pallas import tpu as pltpu
from jax.sharding import PartitionSpec as P

EXPERTS = 64
TASKS = 3
INNER = 256
LANES = 128
ROWS = 16
VMEM_BYTES = 56 * 2**20
F32 = jnp.float32
BF16 = jnp.bfloat16


def params():
    return pltpu.CompilerParams(vmem_limit_bytes=VMEM_BYTES)


def dot_nt(a, b):
    return lax.dot_general(a, b, (((1,), (1,)), ((), ())), preferred_element_type=F32)


def dot_nn(a, b):
    return jnp.dot(a, b, preferred_element_type=F32)


def tables(length):
    outer = length // INNER

    def angles(rows, cols, points):
        product = np.outer(np.arange(rows), np.arange(cols)) % points
        return product * (2.0 * np.pi / points)

    first = angles(outer, outer, outer)
    inner = angles(INNER, INNER, INNER)
    turn = angles(outer, INNER, length)
    c1, s1, c2, s2 = np.cos(first), np.sin(first), np.cos(inner), np.sin(inner)
    f1 = np.concatenate([c1, -s1], 0)
    m2 = np.block([[c2, s2], [-s2, c2]])
    m3 = np.block([[c2, -s2], [s2, c2]])
    f4 = np.concatenate([c1, -s1], 1) / length
    def bf(a):
        near = a.astype(jnp.bfloat16)
        rest = (a - near.astype(np.float64)).astype(jnp.bfloat16)
        return jnp.asarray(np.stack([near, rest]))

    fl = lambda a: jnp.asarray(a.astype(np.float32))
    return (
        bf(f1), bf(m2), bf(m3), bf(f4),
        fl(np.cos(turn)), fl(np.sin(turn)), fl(np.cos(turn).T), fl(np.sin(turn).T),
    )


def turn_kernel(blocks, parts, x_ref, size_ref, *refs):
    outs, low, high = refs[:parts], refs[parts], refs[parts + 1]

    def step(j, _):
        rows = x_ref[pl.ds(pl.multiple_of(j * INNER, INNER), INNER), :]
        turned = rows.astype(F32).T
        low[pl.ds(j, LANES, stride=blocks), :] = turned[:, :LANES]
        high[pl.ds(j, LANES, stride=blocks), :] = turned[:, LANES:]
        return 0

    lax.fori_loop(0, blocks, step, 0, unroll=2)
    dests, rows, _ = outs[0].shape
    rows -= blocks
    counts = jnp.concatenate([size_ref[:1, :], jnp.zeros((1, INNER - LANES), jnp.int32)], 1)
    counts = jnp.broadcast_to(counts.astype(F32), (dests * blocks, INNER)).astype(BF16)
    outs[0][:, rows:, :] = counts.reshape(dests, blocks, INNER)
    for part in range(parts):
        for side, half in enumerate((low, high)):
            value = half[...].reshape(dests, parts, rows, LANES)[:, part]
            outs[part][:, :rows, side * LANES:(side + 1) * LANES] = value.astype(BF16)


def turn(events, size, chan_dev, parts):
    tokens, channels = events.shape
    blocks = tokens // INNER
    rows = chan_dev // parts * blocks
    heights = [rows + blocks] + [rows] * (parts - 1)
    dests = LANES // chan_dev
    return pl.pallas_call(
        functools.partial(turn_kernel, blocks, parts),
        grid=(channels // LANES,),
        in_specs=[
            pl.BlockSpec((tokens, LANES), lambda i: (0, i)),
            pl.BlockSpec(size.shape, lambda i: (0, 0)),
        ],
        out_specs=[pl.BlockSpec((dests, height, INNER), lambda i: (i, 0, 0)) for height in heights],
        out_shape=[
            jax.ShapeDtypeStruct((channels // chan_dev, height, INNER), BF16) for height in heights
        ],
        scratch_shapes=[pltpu.VMEM((LANES * blocks, LANES), F32)] * 2,
        compiler_params=params(),
        name="turn",
    )(events, size)


def spectral_kernel(
    chans, outer, x_ref, h_ref, f1_ref, m2_ref, m3_ref, f4_ref, tc, ts, tct, tst, out_ref,
    y_ref, g_ref,
):
    x_all = x_ref[...]
    for c in range(chans):
        x = x_all[:, c].reshape(outer, INNER)
        a = dot_nn(f1_ref[0], x) + dot_nn(f1_ref[1], x)
        re, im = a[:outer], a[outer:]
        rows = slice(c * outer, (c + 1) * outer)
        y_ref[rows, :INNER] = (re * tc[...] + im * ts[...]).astype(BF16)
        y_ref[rows, INNER:] = (im * tc[...] - re * ts[...]).astype(BF16)
    y_all = y_ref[...]
    z = dot_nt(m2_ref[0], y_all) + dot_nt(m2_ref[1], y_all)
    for c in range(chans):
        cols = slice(c * outer, (c + 1) * outer)
        zr, zi = z[:INNER, cols], z[INNER:, cols]
        hr, hi = h_ref[0, c], h_ref[1, c]
        g_ref[:INNER, cols] = (zr * hr - zi * hi).astype(BF16)
        g_ref[INNER:, cols] = (zr * hi + zi * hr).astype(BF16)
    g_all = g_ref[...]
    u = dot_nn(m3_ref[0], g_all) + dot_nn(m3_ref[1], g_all)
    for c in range(chans):
        cols = slice(c * outer, (c + 1) * outer)
        ur, ui = u[:INNER, cols], u[INNER:, cols]
        v = jnp.concatenate(
            [
                (ur * tct[...] - ui * tst[...]).astype(BF16),
                (ui * tct[...] + ur * tst[...]).astype(BF16),
            ],
            1,
        )
        y = dot_nt(f4_ref[0], v) + dot_nt(f4_ref[1], v)
        x = x_all[:, c].reshape(outer, INNER)
        total = (x.astype(F32) + y).astype(BF16)
        out_ref[:, c] = total.reshape(out_ref.shape[0], out_ref.shape[2], INNER)


def spectral(x, filt, part, chan_dev):
    parts, _, blocks, _ = x.shape
    length = parts * blocks * INNER
    outer = length // INNER
    chans = math.gcd(chan_dev, 4)
    consts = tables(length)
    first = part * (chan_dev // chans)
    whole = lambda a: pl.BlockSpec(a.shape, lambda i: (0,) * a.ndim)
    x_spec = pl.BlockSpec((parts, chans, blocks, INNER), lambda i: (0, i, 0, 0))
    return pl.pallas_call(
        functools.partial(spectral_kernel, chans, outer),
        grid=(chan_dev // chans,),
        in_specs=[x_spec, pl.BlockSpec((2, chans, INNER, outer), lambda i: (0, first + i, 0, 0))]
        + [whole(a) for a in consts],
        out_specs=x_spec,
        out_shape=jax.ShapeDtypeStruct((parts, chan_dev, blocks, INNER), BF16),
        scratch_shapes=[
            pltpu.VMEM((chans * outer, 2 * INNER), BF16),
            pltpu.VMEM((2 * INNER, chans * outer), BF16),
        ],
        compiler_params=params(),
        cost_estimate=pl.CostEstimate(
            flops=chan_dev * 2 * 2 * (2 * outer * outer * INNER * 2 + 8 * INNER * INNER * outer),
            bytes_accessed=chan_dev * length * 12,
            transcendentals=0,
        ),
        name="spectral",
    )(x, filt, *consts)


def slot_kernel(exp_dev, reach, routes_ref, slot_ref, size_ref):
    tokens = routes_ref.shape[1]
    row = lax.broadcasted_iota(jnp.int32, (INNER, INNER), 0)
    col = lax.broadcasted_iota(jnp.int32, (INNER, INNER), 1)
    before = (row < col).astype(F32).astype(BF16)
    expert = lax.broadcasted_iota(jnp.int32, (EXPERTS, INNER), 0)

    def hot_of(j):
        return (expert == routes_ref[:, j * INNER:(j + 1) * INNER]).astype(F32)

    count = jnp.zeros((EXPERTS, 1), F32)
    for j in range(tokens // INNER):
        count = count + jnp.sum(hot_of(j), 1, keepdims=True)
    wide = jnp.broadcast_to(count, (EXPERTS, LANES))
    lanes = jnp.concatenate([wide, jnp.zeros((LANES - EXPERTS, LANES), F32)], 0).T
    size_ref[...] = lanes[:size_ref.shape[0]].astype(jnp.int32)
    mine = lax.broadcasted_iota(jnp.int32, (EXPERTS, EXPERTS), 0)
    other = lax.broadcasted_iota(jnp.int32, (EXPERTS, EXPERTS), 1)
    same = lax.div(mine, exp_dev) == lax.div(other, exp_dev)
    earlier = jnp.where(same & (other < mine), 1.0, 0.0).astype(BF16)
    offset = dot_nn(earlier, wide.astype(BF16))[:, :1]
    owner = lax.div(lax.broadcasted_iota(jnp.int32, (EXPERTS, 1), 0), exp_dev)
    base = offset + (owner * reach).astype(F32)
    for j in range(tokens // INNER):
        hot = hot_of(j)
        rank = dot_nn(hot.astype(BF16), before)
        value = jnp.sum(hot * (rank + base), 0, keepdims=True)
        slot_ref[:, j * INNER:(j + 1) * INNER] = value.astype(jnp.int32)
        base = base + jnp.sum(hot, 1, keepdims=True)


def slots_of(routes, exp_dev, reach):
    return pl.pallas_call(
        functools.partial(slot_kernel, exp_dev, reach),
        out_shape=[
            jax.ShapeDtypeStruct(routes.shape, jnp.int32),
            jax.ShapeDtypeStruct((8, LANES), jnp.int32),
        ],
        compiler_params=params(),
        name="slots",
    )(routes)


def inverse_kernel(slot_ref, out_ref):
    tokens = slot_ref.shape[1]

    def clear(i, _):
        for u in range(16):
            out_ref[0, i * 16 + u] = tokens
        return 0

    lax.fori_loop(0, out_ref.shape[1] // 16, clear, 0)

    def name(i, _):
        places = [slot_ref[0, i * 16 + u] for u in range(16)]
        for u in range(16):
            out_ref[0, places[u]] = i * 16 + u
        return 0

    lax.fori_loop(0, tokens // 16, name, 0)


def inverse_of(slot, slot_total):
    smem = pl.BlockSpec(memory_space=pltpu.SMEM)
    return pl.pallas_call(
        inverse_kernel,
        in_specs=[smem],
        out_specs=smem,
        out_shape=jax.ShapeDtypeStruct((1, slot_total), jnp.int32),
        compiler_params=params(),
        cost_estimate=pl.CostEstimate(
            flops=0, bytes_accessed=slot_total * 1024, transcendentals=0
        ),
        name="inverse",
    )(slot)


def norm_kernel(
    blocks, parts, chunks, *refs
):
    x_refs, refs = refs[:parts], refs[parts:]
    gain_ref, gw_ref, routes_ref, gi_ref, slot_ref, table_ref, *refs = refs
    out_refs, refs = refs[:chunks], refs[chunks:]
    gate_ref, low, high, rows_ref, spread_low, spread_high = refs
    channels = gain_ref.shape[1]
    sources, rows, _ = x_refs[0].shape
    for source in range(sources):
        for part in range(parts):
            x = x_refs[part][source].astype(F32)
            at = pl.ds((source * parts + part) * rows, rows)
            low[at, :] = x[:, :LANES]
            high[at, :] = x[:, LANES:]
    expert = lax.broadcasted_iota(jnp.int32, (EXPERTS, INNER), 0)

    def step(j, _):
        start = pl.multiple_of(j * INNER, INNER)
        t = jnp.concatenate(
            [
                low[pl.ds(j, channels, stride=blocks), :],
                high[pl.ds(j, channels, stride=blocks), :],
            ],
            1,
        )
        centre = jnp.sum(t, 0, keepdims=True) * (1.0 / channels)
        away = t - centre
        var = jnp.sum(away * away, 0, keepdims=True) * (1.0 / channels)
        scaled = away * lax.rsqrt(var + 1e-05)
        normed = (scaled.T * gain_ref[...]).astype(BF16)
        rows_ref[...] = normed.astype(F32)
        scores = dot_nt(gw_ref[...], normed)
        hot = expert == routes_ref[:, pl.ds(start, INNER)]
        for task in range(TASKS):
            part = scores[task * EXPERTS:(task + 1) * EXPERTS]
            chosen = jnp.sum(jnp.where(hot, part, 0.0), 0, keepdims=True)
            index = gi_ref[task:task + 1, pl.ds(start, INNER)]
            bias = jnp.zeros((1, INNER), F32)
            for entry in range(table_ref.shape[1]):
                bias = jnp.where(index == entry, table_ref[task, entry], bias)
            logit = chosen.astype(BF16).astype(F32) + bias
            gate_ref[task:task + 1, pl.ds(start, INNER)] = jax.nn.sigmoid(logit)

        def move(i, _):
            first = pl.multiple_of(i * 16, 16)
            places = [slot_ref[0, start + first + u] for u in range(16)]
            rows = rows_ref[pl.ds(first, 16), :]
            for u in range(16):
                spread_low[pl.ds(places[u], 1), :] = rows[u:u + 1, :LANES]
                spread_high[pl.ds(places[u], 1), :] = rows[u:u + 1, LANES:]
            return 0

        lax.fori_loop(0, INNER // 16, move, 0)
        return 0

    lax.fori_loop(0, blocks, step, 0)
    size = spread_low.shape[0] // chunks
    for chunk in range(chunks):
        rows = slice(chunk * size, (chunk + 1) * size)
        out_refs[chunk][:, :LANES] = spread_low[rows, :].astype(BF16)
        out_refs[chunk][:, LANES:] = spread_high[rows, :].astype(BF16)


def norm_and_send(xs, gain, gate_cols, routes, index, slot, table, slot_total, chunks):
    channels = gain.shape[1]
    parts = len(xs)
    tokens = routes.shape[1]
    blocks = tokens // INNER
    vmem = pl.BlockSpec(memory_space=pltpu.VMEM)
    smem = pl.BlockSpec(memory_space=pltpu.SMEM)
    return pl.pallas_call(
        functools.partial(norm_kernel, blocks, parts, chunks),
        in_specs=[vmem] * (parts + 4) + [smem] * 2,
        out_specs=[vmem] * (chunks + 1),
        out_shape=[jax.ShapeDtypeStruct((slot_total // chunks, channels), BF16)] * chunks
        + [jax.ShapeDtypeStruct((8, tokens), F32)],
        scratch_shapes=[
            pltpu.VMEM((channels * blocks, LANES), F32),
            pltpu.VMEM((channels * blocks, LANES), F32),
            pltpu.VMEM((INNER, channels), F32),
            pltpu.VMEM((slot_total, LANES), F32),
            pltpu.VMEM((slot_total, LANES), F32),
        ],
        compiler_params=params(),
        name="norm",
    )(*xs, gain, gate_cols, routes, index, slot, table)


def expert_kernel(chunk, x_ref, w_in_ref, w_out_ref, start_ref, size_ref, out_ref, held, made):
    e = pl.program_id(0)
    sources, height, channels = x_ref.shape

    def piece(source):
        start = start_ref[source, e] - chunk * height
        low = jnp.clip(start, 0, height)
        high = jnp.clip(start + size_ref[source, e], 0, height)
        first = lax.div(low, ROWS)
        count = jnp.where(high > low, lax.div(high + (ROWS - 1), ROWS) - first, 0)
        return low, high, first * ROWS, count

    def at(first, i):
        return pl.ds(pl.multiple_of(first + i * ROWS, ROWS), ROWS)

    def fetch(source, filled):
        _, _, first, count = piece(source)

        def one(i, _):
            held[at(filled, i), :] = x_ref[source, at(first, i), :]
            return 0

        lax.fori_loop(0, count, one, 0)
        return filled + count * ROWS

    total = lax.fori_loop(0, sources, fetch, 0)
    w_in = w_in_ref[...].reshape(-1, channels)
    w_out = w_out_ref[...].reshape(-1, channels)

    def tile(t, _):
        rows = pl.ds(pl.multiple_of(t * INNER, INNER), INNER)
        hidden = jnp.maximum(dot_nt(held[rows, :], w_in), 0.0).astype(BF16)
        made[rows, :] = dot_nn(hidden, w_out).astype(BF16)
        return 0

    lax.fori_loop(0, lax.div(total + INNER - 1, INNER), tile, 0)

    offset = lax.broadcasted_iota(jnp.int32, (ROWS, channels), 0)

    def give(source, filled):
        low, high, first, count = piece(source)

        def one(i, _):
            row = offset + (first + i * ROWS)
            new = made[at(filled, i), :].astype(F32)
            old = out_ref[source, at(first, i), :].astype(F32)
            mine = (row >= low) & (row < high)
            out_ref[source, at(first, i), :] = jnp.where(mine, new, old).astype(BF16)
            return 0

        lax.fori_loop(0, count, one, 0)
        return filled + count * ROWS

    lax.fori_loop(0, sources, give, 0)


def experts(x, w_in, w_out, start, size, chunk, chunks, capacity):
    sources, height, channels = x.shape
    shares, count, hid, _ = w_in.shape
    most = -(-sources * (capacity + 2 * ROWS) // INNER) * INNER
    x_spec = pl.BlockSpec(x.shape, lambda e: (0, 0, 0))
    w_spec = pl.BlockSpec((shares, 1, hid, channels), lambda e: (0, e, 0, 0))
    flat_spec = pl.BlockSpec((shares, hid, channels), lambda e: (0, e, 0))
    smem = pl.BlockSpec(memory_space=pltpu.SMEM)
    return pl.pallas_call(
        functools.partial(expert_kernel, chunk),
        grid=(count,),
        in_specs=[x_spec, w_spec, flat_spec, smem, smem],
        out_specs=x_spec,
        out_shape=jax.ShapeDtypeStruct(x.shape, BF16),
        scratch_shapes=[pltpu.VMEM((most, channels), BF16)] * 2,
        compiler_params=params(),
        cost_estimate=pl.CostEstimate(
            flops=4 * sources * height * channels * shares * hid,
            bytes_accessed=2 * (2 * x.size + w_in.size + w_out.size),
            transcendentals=0,
        ),
        name="experts",
    )(x, w_in, w_out, start, size)


def scatter_rows(chunk, reach, res_ref, inverse_ref, total_ref, wide, low, high):
    owners = total_ref.shape[1]
    height = res_ref.shape[0] // owners
    wide[...] = res_ref[...].astype(F32)

    def owner_rows(owner, _):
        count = jnp.clip(total_ref[0, owner] - chunk * height, 0, height)
        slots = owner * reach + chunk * height

        def move(i, _):
            first = i * 16
            events = [inverse_ref[0, slots + first + u] for u in range(16)]
            rows = wide[pl.ds(pl.multiple_of(owner * height + first, 16), 16), :]
            for u in range(16):
                low[pl.ds(events[u], 1), :] = rows[u:u + 1, :LANES]
                high[pl.ds(events[u], 1), :] = rows[u:u + 1, LANES:]
            return 0

        lax.fori_loop(0, lax.div(count + 15, 16), move, 0)
        return 0

    lax.fori_loop(0, owners, owner_rows, 0)


def put_back_kernel(chunk, reach, base, res_ref, inverse_ref, total_ref, *refs):
    old, (low, high, wide) = refs[:base], refs[base:]
    for source, target in zip(old, (low, high)):
        target[...] = source[...]
    scatter_rows(chunk, reach, res_ref, inverse_ref, total_ref, wide, low, high)


def put_back(base, res, inverse, totals, chunk, reach, tokens):
    vmem = pl.BlockSpec(memory_space=pltpu.VMEM)
    smem = pl.BlockSpec(memory_space=pltpu.SMEM)
    return pl.pallas_call(
        functools.partial(put_back_kernel, chunk, reach, len(base)),
        in_specs=[vmem, smem, smem] + [vmem] * len(base),
        out_specs=[vmem, vmem],
        out_shape=[jax.ShapeDtypeStruct((tokens + 8, LANES), F32)] * 2,
        scratch_shapes=[pltpu.VMEM(res.shape, F32)],
        compiler_params=params(),
        cost_estimate=pl.CostEstimate(
            flops=0, bytes_accessed=res.size * 16, transcendentals=0
        ),
        name="put_back",
    )(res, inverse, totals, *base)


def finish_kernel(chunk, reach, base, res_ref, inverse_ref, total_ref, gate_ref, *refs):
    old, (out_ref, wide, low, high) = refs[:base], refs[base:]
    j = pl.program_id(0)

    @pl.when(j == 0)
    def _():
        for source, target in zip(old, (low, high)):
            target[...] = source[...]
        scatter_rows(chunk, reach, res_ref, inverse_ref, total_ref, wide, low, high)

    block = pl.ds(pl.multiple_of(j * INNER, INNER), INNER)
    gates = gate_ref[...].T
    for side, half in enumerate((low, high)):
        rows = half[block, :]
        for task in range(TASKS):
            value = (gates[:, task:task + 1] * rows).astype(BF16)
            out_ref[task, :, side * LANES:(side + 1) * LANES] = value


def finish(base, res, gates, inverse, totals, chunk, reach):
    tokens = gates.shape[1]
    channels = res.shape[1]
    smem = pl.BlockSpec(memory_space=pltpu.SMEM)
    return pl.pallas_call(
        functools.partial(finish_kernel, chunk, reach, len(base)),
        grid=(tokens // INNER,),
        in_specs=[
            pl.BlockSpec(res.shape, lambda j: (0, 0)),
            smem,
            smem,
            pl.BlockSpec((8, INNER), lambda j: (0, j)),
        ]
        + [pl.BlockSpec(a.shape, lambda j: (0, 0)) for a in base],
        out_specs=pl.BlockSpec((TASKS, INNER, channels), lambda j: (0, j, 0)),
        out_shape=jax.ShapeDtypeStruct((TASKS, tokens, channels), BF16),
        scratch_shapes=[
            pltpu.VMEM(res.shape, F32),
            pltpu.VMEM((tokens + 8, LANES), F32),
            pltpu.VMEM((tokens + 8, LANES), F32),
        ],
        compiler_params=params(),
        name="finish",
    )(res, inverse, totals, gates, *base)


def on_device(
    events, spectral_filter, ln_gain, w_in, w_out, gate_weight, gate_table, routes, gate_index
):
    n_seq = lax.axis_size("seq")
    _, len_dev, user_count, channels = events.shape
    chan_dev = channels // n_seq
    blocks = len_dev // INNER
    capacity = max(2, 2 * len_dev // EXPERTS)
    exp_dev = w_in.shape[0]
    reach = exp_dev * capacity
    parts = 2 if chan_dev % 16 == 0 and blocks % 16 == 0 else 1
    route_row = routes.reshape(1, len_dev)
    index_rows = gate_index.reshape(len_dev, TASKS).T
    gate_cols = gate_weight.transpose(0, 2, 1).reshape(TASKS * EXPERTS, channels)

    slot, size = slots_of(route_row, exp_dev, reach)
    inverse = inverse_of(slot, n_seq * reach)
    totals = jnp.sum(size[0, :EXPERTS].reshape(1, n_seq, exp_dev), -1)
    all_in = lax.all_gather(w_in, "batch", axis=0, tiled=False)
    turned_parts = turn(events.reshape(len_dev, channels), size, chan_dev, parts)

    length = len_dev * n_seq
    filt = spectral_filter.transpose(0, 2, 1).reshape(2, chan_dev, INNER, length // INNER)
    chan_part = chan_dev // parts
    returned = []
    for part, turned in enumerate(turned_parts):
        history = lax.all_to_all(turned, "seq", split_axis=0, concat_axis=0, tiled=True)
        history = history.reshape(n_seq, -1, blocks, INNER)
        if part == 0:
            counts = history[:, chan_part, 0, :EXPERTS].astype(jnp.int32)
        if blocks % 16:
            merged = history[:, :chan_part].transpose(1, 0, 2, 3)
            merged = merged.reshape(1, chan_part, n_seq * blocks, INNER)
            summed = spectral(merged, filt, part, chan_part)
            summed = summed.reshape(chan_part, n_seq, blocks, INNER).transpose(1, 0, 2, 3)
        else:
            summed = spectral(history, filt, part, chan_part)
        summed = summed.reshape(n_seq, chan_part * blocks, INNER)
        returned.append(
            lax.all_to_all(summed, "seq", split_axis=0, concat_axis=0, tiled=True)
        )

    heights = tier_heights(reach)
    tallest = jnp.max(jnp.sum(counts.reshape(n_seq, n_seq, exp_dev), -1))
    tier = sum((tallest > height).astype(F32) for height in heights[:-1]) + jnp.zeros((), F32)
    tail = jnp.broadcast_to(tier.astype(BF16), (ROWS, channels))
    hid = w_out.shape[1]
    with_tier = jnp.concatenate([w_out.reshape(exp_dev * hid, channels), tail], 0)
    all_out = lax.all_gather(with_tier, "batch", axis=0, tiled=False)
    tier = jnp.max(all_out[:, exp_dev * hid, 0].astype(F32)).astype(jnp.int32)
    own = lax.dynamic_slice(counts, (0, lax.axis_index("seq") * exp_dev), (n_seq, exp_dev))
    ahead = jnp.arange(exp_dev)[:, None] > jnp.arange(exp_dev)[None, :]
    start = jnp.sum(jnp.where(ahead[None], own[:, None, :], 0), -1)

    def mixture(height, returned, slot, inverse, totals, start, own, all_in, all_out):
        chunks = 2 if height % (2 * ROWS) == 0 else 1
        chunk_rows = height // chunks
        owner, local = slot // reach, slot % reach
        chunk_of = local // chunk_rows
        place = (chunk_of * n_seq + owner) * chunk_rows + local % chunk_rows
        *outgoing, gates = norm_and_send(
            returned,
            ln_gain.reshape(1, channels),
            gate_cols,
            route_row,
            index_rows,
            place,
            gate_table,
            n_seq * height,
            chunks,
        )
        results = []
        for chunk, rows in enumerate(outgoing):
            arrived = lax.all_to_all(
                rows.reshape(n_seq, chunk_rows, channels),
                "seq", split_axis=0, concat_axis=0, tiled=True,
            )
            done = experts(arrived, all_in, all_out, start, own, chunk, chunks, capacity)
            back = lax.all_to_all(done, "seq", split_axis=0, concat_axis=0, tiled=True)
            back = back.reshape(n_seq * chunk_rows, channels)
            if chunk < chunks - 1:
                results = put_back(results, back, inverse, totals, chunk, reach, len_dev)
        return finish(results, back, gates, inverse, totals, chunks - 1, reach)

    branches = [functools.partial(mixture, height) for height in heights]
    task_out = lax.switch(
        tier, branches, returned, slot, inverse, totals, start, own, all_in, all_out
    )
    return task_out.reshape(TASKS, 1, len_dev, user_count, channels)


def tier_heights(reach):
    if reach % 1024:
        return [reach]
    return [reach // 32 * share for share in (21, 22, 23, 24, 25, 26, 28, 32)]


def solution(mesh):
    in_specs = (
        P("batch", "seq", None, None),
        P(None, None, "seq"),
        P(),
        P("seq", "batch", None),
        P("seq", "batch", None),
        P(),
        P(),
        P("batch", "seq", None, None),
        P("batch", "seq", None, None),
    )
    out_specs = P(None, "batch", "seq", None, None)
    return jax.shard_map(
        on_device, mesh=mesh, in_specs=in_specs, out_specs=out_specs, check_vma=False
    )
```

```python
import functools
import math

import jax
import jax.numpy as jnp
import numpy as np
from jax import lax
from jax.experimental import pallas as pl
from jax.experimental.pallas import tpu as pltpu
from jax.sharding import PartitionSpec as P

EXPERTS = 64
TASKS = 3
INNER = 256
LANES = 128
ROWS = 16
VMEM_BYTES = 56 * 2**20
F32 = jnp.float32
BF16 = jnp.bfloat16


def params():
    return pltpu.CompilerParams(vmem_limit_bytes=VMEM_BYTES)


def dot_nt(a, b):
    return lax.dot_general(a, b, (((1,), (1,)), ((), ())), preferred_element_type=F32)


def dot_nn(a, b):
    return jnp.dot(a, b, preferred_element_type=F32)


def tables(length):
    outer = length // INNER

    def angles(rows, cols, points):
        product = np.outer(np.arange(rows), np.arange(cols)) % points
        return product * (2.0 * np.pi / points)

    first = angles(outer, outer, outer)
    inner = angles(INNER, INNER, INNER)
    turn = angles(outer, INNER, length)
    c1, s1, c2, s2 = np.cos(first), np.sin(first), np.cos(inner), np.sin(inner)
    f1 = np.concatenate([c1, -s1], 0)
    m2 = np.block([[c2, s2], [-s2, c2]])
    m3 = np.block([[c2, -s2], [s2, c2]])
    f4 = np.concatenate([c1, -s1], 1) / length
    def bf(a):
        near = a.astype(jnp.bfloat16)
        rest = (a - near.astype(np.float64)).astype(jnp.bfloat16)
        return jnp.asarray(np.stack([near, rest]))

    fl = lambda a: jnp.asarray(a.astype(np.float32))
    return (
        bf(f1), bf(m2), bf(m3), bf(f4),
        fl(np.cos(turn)), fl(np.sin(turn)), fl(np.cos(turn).T), fl(np.sin(turn).T),
    )


def turn_kernel(blocks, parts, part, x_ref, size_ref, *refs):
    out, low, high = refs[-3:]

    def step(j, _):
        rows = x_ref[pl.ds(pl.multiple_of(j * INNER, INNER), INNER), :]
        turned = rows.astype(F32).T
        low[pl.ds(j, LANES, stride=blocks), :] = turned[:, :LANES]
        high[pl.ds(j, LANES, stride=blocks), :] = turned[:, LANES:]
        return 0

    lax.fori_loop(0, blocks, step, 0, unroll=2)
    dests, rows, _ = out.shape
    if part == 0:
        rows -= blocks
        counts = jnp.concatenate([size_ref[:1, :], jnp.zeros((1, INNER - LANES), jnp.int32)], 1)
        counts = jnp.broadcast_to(counts.astype(F32), (dests * blocks, INNER)).astype(BF16)
        out[:, rows:, :] = counts.reshape(dests, blocks, INNER)
    for side, half in enumerate((low, high)):
        value = half[...].reshape(dests, parts, rows, LANES)[:, part]
        out[:, :rows, side * LANES:(side + 1) * LANES] = value.astype(BF16)


def turn(events, size, chan_dev, parts, part, *after):
    tokens, channels = events.shape
    blocks = tokens // INNER
    rows = chan_dev // parts * blocks
    height = rows + blocks if part == 0 else rows
    dests = LANES // chan_dev
    return pl.pallas_call(
        functools.partial(turn_kernel, blocks, parts, part),
        grid=(channels // LANES,),
        in_specs=[
            pl.BlockSpec((tokens, LANES), lambda i: (0, i)),
            pl.BlockSpec(size.shape, lambda i: (0, 0)),
        ]
        + [pl.BlockSpec(memory_space=pl.ANY)] * len(after),
        out_specs=pl.BlockSpec((dests, height, INNER), lambda i: (i, 0, 0)),
        out_shape=jax.ShapeDtypeStruct((channels // chan_dev, height, INNER), BF16),
        scratch_shapes=[pltpu.VMEM((LANES * blocks, LANES), F32)] * 2,
        compiler_params=params(),
        name="turn",
    )(events, size, *after)


def spectral_kernel(
    chans, outer, x_ref, h_ref, f1_ref, m2_ref, m3_ref, f4_ref, tc, ts, tct, tst, out_ref,
    y_ref, g_ref,
):
    x_all = x_ref[...]
    for c in range(chans):
        x = x_all[:, c].reshape(outer, INNER)
        a = dot_nn(f1_ref[0], x) + dot_nn(f1_ref[1], x)
        re, im = a[:outer], a[outer:]
        rows = slice(c * outer, (c + 1) * outer)
        y_ref[rows, :INNER] = (re * tc[...] + im * ts[...]).astype(BF16)
        y_ref[rows, INNER:] = (im * tc[...] - re * ts[...]).astype(BF16)
    y_all = y_ref[...]
    z = dot_nt(m2_ref[0], y_all) + dot_nt(m2_ref[1], y_all)
    for c in range(chans):
        cols = slice(c * outer, (c + 1) * outer)
        zr, zi = z[:INNER, cols], z[INNER:, cols]
        hr, hi = h_ref[0, c], h_ref[1, c]
        g_ref[:INNER, cols] = (zr * hr - zi * hi).astype(BF16)
        g_ref[INNER:, cols] = (zr * hi + zi * hr).astype(BF16)
    g_all = g_ref[...]
    u = dot_nn(m3_ref[0], g_all) + dot_nn(m3_ref[1], g_all)
    for c in range(chans):
        cols = slice(c * outer, (c + 1) * outer)
        ur, ui = u[:INNER, cols], u[INNER:, cols]
        v = jnp.concatenate(
            [
                (ur * tct[...] - ui * tst[...]).astype(BF16),
                (ui * tct[...] + ur * tst[...]).astype(BF16),
            ],
            1,
        )
        y = dot_nt(f4_ref[0], v) + dot_nt(f4_ref[1], v)
        x = x_all[:, c].reshape(outer, INNER)
        total = (x.astype(F32) + y).astype(BF16)
        out_ref[:, c] = total.reshape(out_ref.shape[0], out_ref.shape[2], INNER)


def spectral(x, filt, part, chan_dev):
    parts, _, blocks, _ = x.shape
    length = parts * blocks * INNER
    outer = length // INNER
    chans = math.gcd(chan_dev, 4)
    consts = tables(length)
    first = part * (chan_dev // chans)
    whole = lambda a: pl.BlockSpec(a.shape, lambda i: (0,) * a.ndim)
    x_spec = pl.BlockSpec((parts, chans, blocks, INNER), lambda i: (0, i, 0, 0))
    return pl.pallas_call(
        functools.partial(spectral_kernel, chans, outer),
        grid=(chan_dev // chans,),
        in_specs=[x_spec, pl.BlockSpec((2, chans, INNER, outer), lambda i: (0, first + i, 0, 0))]
        + [whole(a) for a in consts],
        out_specs=x_spec,
        out_shape=jax.ShapeDtypeStruct((parts, chan_dev, blocks, INNER), BF16),
        scratch_shapes=[
            pltpu.VMEM((chans * outer, 2 * INNER), BF16),
            pltpu.VMEM((2 * INNER, chans * outer), BF16),
        ],
        compiler_params=params(),
        cost_estimate=pl.CostEstimate(
            flops=chan_dev * 2 * 2 * (2 * outer * outer * INNER * 2 + 8 * INNER * INNER * outer),
            bytes_accessed=chan_dev * length * 12,
            transcendentals=0,
        ),
        name="spectral",
    )(x, filt, *consts)


def slot_kernel(exp_dev, reach, routes_ref, slot_ref, size_ref):
    tokens = routes_ref.shape[1]
    row = lax.broadcasted_iota(jnp.int32, (INNER, INNER), 0)
    col = lax.broadcasted_iota(jnp.int32, (INNER, INNER), 1)
    before = (row < col).astype(F32).astype(BF16)
    expert = lax.broadcasted_iota(jnp.int32, (EXPERTS, INNER), 0)

    def hot_of(j):
        return (expert == routes_ref[:, j * INNER:(j + 1) * INNER]).astype(F32)

    count = jnp.zeros((EXPERTS, 1), F32)
    for j in range(tokens // INNER):
        count = count + jnp.sum(hot_of(j), 1, keepdims=True)
    wide = jnp.broadcast_to(count, (EXPERTS, LANES))
    lanes = jnp.concatenate([wide, jnp.zeros((LANES - EXPERTS, LANES), F32)], 0).T
    size_ref[...] = lanes[:size_ref.shape[0]].astype(jnp.int32)
    mine = lax.broadcasted_iota(jnp.int32, (EXPERTS, EXPERTS), 0)
    other = lax.broadcasted_iota(jnp.int32, (EXPERTS, EXPERTS), 1)
    same = lax.div(mine, exp_dev) == lax.div(other, exp_dev)
    earlier = jnp.where(same & (other < mine), 1.0, 0.0).astype(BF16)
    offset = dot_nn(earlier, wide.astype(BF16))[:, :1]
    owner = lax.div(lax.broadcasted_iota(jnp.int32, (EXPERTS, 1), 0), exp_dev)
    base = offset + (owner * reach).astype(F32)
    for j in range(tokens // INNER):
        hot = hot_of(j)
        rank = dot_nn(hot.astype(BF16), before)
        value = jnp.sum(hot * (rank + base), 0, keepdims=True)
        slot_ref[:, j * INNER:(j + 1) * INNER] = value.astype(jnp.int32)
        base = base + jnp.sum(hot, 1, keepdims=True)


def slots_of(routes, exp_dev, reach):
    return pl.pallas_call(
        functools.partial(slot_kernel, exp_dev, reach),
        out_shape=[
            jax.ShapeDtypeStruct(routes.shape, jnp.int32),
            jax.ShapeDtypeStruct((8, LANES), jnp.int32),
        ],
        compiler_params=params(),
        name="slots",
    )(routes)


def inverse_kernel(slot_ref, after_ref, out_ref):
    tokens = slot_ref.shape[1]

    def clear(i, _):
        for u in range(16):
            out_ref[0, i * 16 + u] = tokens
        return 0

    lax.fori_loop(0, out_ref.shape[1] // 16, clear, 0)

    def name(i, _):
        places = [slot_ref[0, i * 16 + u] for u in range(16)]
        for u in range(16):
            out_ref[0, places[u]] = i * 16 + u
        return 0

    lax.fori_loop(0, tokens // 16, name, 0)


def inverse_of(slot, slot_total, after):
    smem = pl.BlockSpec(memory_space=pltpu.SMEM)
    return pl.pallas_call(
        inverse_kernel,
        in_specs=[smem, pl.BlockSpec(memory_space=pl.ANY)],
        out_specs=smem,
        out_shape=jax.ShapeDtypeStruct((1, slot_total), jnp.int32),
        compiler_params=params(),
        cost_estimate=pl.CostEstimate(
            flops=0, bytes_accessed=slot_total * 1024, transcendentals=0
        ),
        name="inverse",
    )(slot, after)


def tier_kernel(exp_dev, heights, count_ref, after_ref, out_ref, counts_ref):
    counts = jnp.max(count_ref[:, 0].astype(F32), 1)[:, :EXPERTS]
    counts_ref[...] = counts.astype(jnp.int32)
    expert = lax.broadcasted_iota(jnp.int32, (EXPERTS, LANES), 0)
    owner = lax.broadcasted_iota(jnp.int32, (EXPERTS, LANES), 1)
    same = jnp.where(lax.div(expert, exp_dev) == owner, 1.0, 0.0).astype(BF16)
    loads = dot_nn(counts.astype(BF16), same)
    tallest = jnp.max(jnp.max(loads, 0, keepdims=True), 1, keepdims=True)
    tier = jnp.zeros((1, 1), F32)
    for height in heights[:-1]:
        tier = tier + jnp.where(tallest > height, 1.0, 0.0)
    out_ref[...] = jnp.broadcast_to(tier, out_ref.shape).astype(BF16)


def tier_of(history, row, exp_dev, heights, channels, after):
    sources, _, blocks, _ = history.shape
    whole = lambda shape: pl.BlockSpec(shape, lambda i: (0,) * len(shape))
    return pl.pallas_call(
        functools.partial(tier_kernel, exp_dev, heights),
        grid=(1,),
        in_specs=[
            pl.BlockSpec((sources, 1, blocks, INNER), lambda i: (0, row, 0, 0)),
            pl.BlockSpec(memory_space=pl.ANY),
        ],
        out_specs=[whole((ROWS, channels)), whole((sources, EXPERTS))],
        out_shape=[
            jax.ShapeDtypeStruct((ROWS, channels), BF16),
            jax.ShapeDtypeStruct((sources, EXPERTS), jnp.int32),
        ],
        compiler_params=params(),
        name="tier",
    )(history, after)


def norm_kernel(
    blocks, parts, chunks, *refs
):
    x_refs, refs = refs[:parts], refs[parts:]
    gain_ref, gw_ref, routes_ref, gi_ref, slot_ref, table_ref, *refs = refs
    out_refs, refs = refs[:chunks], refs[chunks:]
    gate_ref, low, high, rows_ref, spread_low, spread_high = refs
    channels = gain_ref.shape[1]
    sources, rows, _ = x_refs[0].shape
    for source in range(sources):
        for part in range(parts):
            x = x_refs[part][source].astype(F32)
            at = pl.ds((source * parts + part) * rows, rows)
            low[at, :] = x[:, :LANES]
            high[at, :] = x[:, LANES:]
    expert = lax.broadcasted_iota(jnp.int32, (EXPERTS, INNER), 0)

    def step(j, _):
        start = pl.multiple_of(j * INNER, INNER)
        t = jnp.concatenate(
            [
                low[pl.ds(j, channels, stride=blocks), :],
                high[pl.ds(j, channels, stride=blocks), :],
            ],
            1,
        )
        centre = jnp.sum(t, 0, keepdims=True) * (1.0 / channels)
        away = t - centre
        var = jnp.sum(away * away, 0, keepdims=True) * (1.0 / channels)
        scaled = away * lax.rsqrt(var + 1e-05)
        normed = (scaled.T * gain_ref[...]).astype(BF16)
        rows_ref[...] = normed.astype(F32)
        scores = dot_nt(gw_ref[...], normed)
        hot = expert == routes_ref[:, pl.ds(start, INNER)]
        for task in range(TASKS):
            part = scores[task * EXPERTS:(task + 1) * EXPERTS]
            chosen = jnp.sum(jnp.where(hot, part, 0.0), 0, keepdims=True)
            index = gi_ref[task:task + 1, pl.ds(start, INNER)]
            bias = jnp.zeros((1, INNER), F32)
            for entry in range(table_ref.shape[1]):
                bias = jnp.where(index == entry, table_ref[task, entry], bias)
            logit = chosen.astype(BF16).astype(F32) + bias
            gate_ref[task:task + 1, pl.ds(start, INNER)] = jax.nn.sigmoid(logit)

        def move(i, _):
            first = pl.multiple_of(i * 16, 16)
            places = [slot_ref[0, start + first + u] for u in range(16)]
            rows = rows_ref[pl.ds(first, 16), :]
            for u in range(16):
                spread_low[pl.ds(places[u], 1), :] = rows[u:u + 1, :LANES]
                spread_high[pl.ds(places[u], 1), :] = rows[u:u + 1, LANES:]
            return 0

        lax.fori_loop(0, INNER // 16, move, 0)
        return 0

    lax.fori_loop(0, blocks, step, 0)
    size = spread_low.shape[0] // chunks
    for chunk in range(chunks):
        rows = slice(chunk * size, (chunk + 1) * size)
        out_refs[chunk][:, :LANES] = spread_low[rows, :].astype(BF16)
        out_refs[chunk][:, LANES:] = spread_high[rows, :].astype(BF16)


def norm_and_send(xs, gain, gate_cols, routes, index, slot, table, slot_total, chunks):
    channels = gain.shape[1]
    parts = len(xs)
    tokens = routes.shape[1]
    blocks = tokens // INNER
    vmem = pl.BlockSpec(memory_space=pltpu.VMEM)
    smem = pl.BlockSpec(memory_space=pltpu.SMEM)
    return pl.pallas_call(
        functools.partial(norm_kernel, blocks, parts, chunks),
        in_specs=[vmem] * (parts + 4) + [smem] * 2,
        out_specs=[vmem] * (chunks + 1),
        out_shape=[jax.ShapeDtypeStruct((slot_total // chunks, channels), BF16)] * chunks
        + [jax.ShapeDtypeStruct((8, tokens), F32)],
        scratch_shapes=[
            pltpu.VMEM((channels * blocks, LANES), F32),
            pltpu.VMEM((channels * blocks, LANES), F32),
            pltpu.VMEM((INNER, channels), F32),
            pltpu.VMEM((slot_total, LANES), F32),
            pltpu.VMEM((slot_total, LANES), F32),
        ],
        compiler_params=params(),
        name="norm",
    )(*xs, gain, gate_cols, routes, index, slot, table)


def expert_kernel(chunk, x_ref, w_in_ref, w_out_ref, start_ref, size_ref, out_ref, held, made):
    e = pl.program_id(0)
    sources, height, channels = x_ref.shape

    def piece(source):
        start = start_ref[source, e] - chunk * height
        low = jnp.clip(start, 0, height)
        high = jnp.clip(start + size_ref[source, e], 0, height)
        first = lax.div(low, ROWS)
        count = jnp.where(high > low, lax.div(high + (ROWS - 1), ROWS) - first, 0)
        return low, high, first * ROWS, count

    def at(first, i):
        return pl.ds(pl.multiple_of(first + i * ROWS, ROWS), ROWS)

    def fetch(source, filled):
        _, _, first, count = piece(source)

        def one(i, _):
            held[at(filled, i), :] = x_ref[source, at(first, i), :]
            return 0

        lax.fori_loop(0, count, one, 0)
        return filled + count * ROWS

    total = lax.fori_loop(0, sources, fetch, 0)
    w_in = w_in_ref[...].reshape(-1, channels)
    w_out = w_out_ref[...].reshape(-1, channels)

    def tile(t, _):
        rows = pl.ds(pl.multiple_of(t * INNER, INNER), INNER)
        hidden = jnp.maximum(dot_nt(held[rows, :], w_in), 0.0).astype(BF16)
        made[rows, :] = dot_nn(hidden, w_out).astype(BF16)
        return 0

    lax.fori_loop(0, lax.div(total + INNER - 1, INNER), tile, 0)

    offset = lax.broadcasted_iota(jnp.int32, (ROWS, channels), 0)

    def give(source, filled):
        low, high, first, count = piece(source)

        def one(i, _):
            row = offset + (first + i * ROWS)
            new = made[at(filled, i), :].astype(F32)
            old = out_ref[source, at(first, i), :].astype(F32)
            mine = (row >= low) & (row < high)
            out_ref[source, at(first, i), :] = jnp.where(mine, new, old).astype(BF16)
            return 0

        lax.fori_loop(0, count, one, 0)
        return filled + count * ROWS

    lax.fori_loop(0, sources, give, 0)


def experts(x, w_in, w_out, start, size, chunk, chunks, capacity):
    sources, height, channels = x.shape
    shares, count, hid, _ = w_in.shape
    most = -(-sources * (capacity + 2 * ROWS) // INNER) * INNER
    x_spec = pl.BlockSpec(x.shape, lambda e: (0, 0, 0))
    w_spec = pl.BlockSpec((shares, 1, hid, channels), lambda e: (0, e, 0, 0))
    flat_spec = pl.BlockSpec((shares, hid, channels), lambda e: (0, e, 0))
    smem = pl.BlockSpec(memory_space=pltpu.SMEM)
    return pl.pallas_call(
        functools.partial(expert_kernel, chunk),
        grid=(count,),
        in_specs=[x_spec, w_spec, flat_spec, smem, smem],
        out_specs=x_spec,
        out_shape=jax.ShapeDtypeStruct(x.shape, BF16),
        scratch_shapes=[pltpu.VMEM((most, channels), BF16)] * 2,
        compiler_params=params(),
        cost_estimate=pl.CostEstimate(
            flops=4 * sources * height * channels * shares * hid,
            bytes_accessed=2 * (2 * x.size + w_in.size + w_out.size),
            transcendentals=0,
        ),
        name="experts",
    )(x, w_in, w_out, start, size)


def scatter_rows(chunk, reach, res_ref, inverse_ref, total_ref, wide, low, high):
    owners = total_ref.shape[1]
    height = res_ref.shape[0] // owners
    wide[...] = res_ref[...].astype(F32)

    def owner_rows(owner, _):
        count = jnp.clip(total_ref[0, owner] - chunk * height, 0, height)
        slots = owner * reach + chunk * height

        def move(i, _):
            first = i * 16
            events = [inverse_ref[0, slots + first + u] for u in range(16)]
            rows = wide[pl.ds(pl.multiple_of(owner * height + first, 16), 16), :]
            for u in range(16):
                low[pl.ds(events[u], 1), :] = rows[u:u + 1, :LANES]
                high[pl.ds(events[u], 1), :] = rows[u:u + 1, LANES:]
            return 0

        lax.fori_loop(0, lax.div(count + 15, 16), move, 0)
        return 0

    lax.fori_loop(0, owners, owner_rows, 0)


def put_back_kernel(chunk, reach, base, res_ref, inverse_ref, total_ref, *refs):
    old, (low, high, wide) = refs[:base], refs[base:]
    for source, target in zip(old, (low, high)):
        target[...] = source[...]
    scatter_rows(chunk, reach, res_ref, inverse_ref, total_ref, wide, low, high)


def put_back(base, res, inverse, totals, chunk, reach, tokens):
    vmem = pl.BlockSpec(memory_space=pltpu.VMEM)
    smem = pl.BlockSpec(memory_space=pltpu.SMEM)
    return pl.pallas_call(
        functools.partial(put_back_kernel, chunk, reach, len(base)),
        in_specs=[vmem, smem, smem] + [vmem] * len(base),
        out_specs=[vmem, vmem],
        out_shape=[jax.ShapeDtypeStruct((tokens + 8, LANES), F32)] * 2,
        scratch_shapes=[pltpu.VMEM(res.shape, F32)],
        compiler_params=params(),
        cost_estimate=pl.CostEstimate(
            flops=0, bytes_accessed=res.size * 16, transcendentals=0
        ),
        name="put_back",
    )(res, inverse, totals, *base)


def finish_kernel(chunk, reach, base, res_ref, inverse_ref, total_ref, gate_ref, *refs):
    old, (out_ref, wide, low, high) = refs[:base], refs[base:]
    j = pl.program_id(0)

    @pl.when(j == 0)
    def _():
        for source, target in zip(old, (low, high)):
            target[...] = source[...]
        scatter_rows(chunk, reach, res_ref, inverse_ref, total_ref, wide, low, high)

    block = pl.ds(pl.multiple_of(j * INNER, INNER), INNER)
    gates = gate_ref[...].T
    for side, half in enumerate((low, high)):
        rows = half[block, :]
        for task in range(TASKS):
            value = (gates[:, task:task + 1] * rows).astype(BF16)
            out_ref[task, :, side * LANES:(side + 1) * LANES] = value


def finish(base, res, gates, inverse, totals, chunk, reach):
    tokens = gates.shape[1]
    channels = res.shape[1]
    smem = pl.BlockSpec(memory_space=pltpu.SMEM)
    return pl.pallas_call(
        functools.partial(finish_kernel, chunk, reach, len(base)),
        grid=(tokens // INNER,),
        in_specs=[
            pl.BlockSpec(res.shape, lambda j: (0, 0)),
            smem,
            smem,
            pl.BlockSpec((8, INNER), lambda j: (0, j)),
        ]
        + [pl.BlockSpec(a.shape, lambda j: (0, 0)) for a in base],
        out_specs=pl.BlockSpec((TASKS, INNER, channels), lambda j: (0, j, 0)),
        out_shape=jax.ShapeDtypeStruct((TASKS, tokens, channels), BF16),
        scratch_shapes=[
            pltpu.VMEM(res.shape, F32),
            pltpu.VMEM((tokens + 8, LANES), F32),
            pltpu.VMEM((tokens + 8, LANES), F32),
        ],
        compiler_params=params(),
        name="finish",
    )(res, inverse, totals, gates, *base)


def on_device(
    events, spectral_filter, ln_gain, w_in, w_out, gate_weight, gate_table, routes, gate_index
):
    n_seq = lax.axis_size("seq")
    _, len_dev, user_count, channels = events.shape
    chan_dev = channels // n_seq
    blocks = len_dev // INNER
    capacity = max(2, 2 * len_dev // EXPERTS)
    exp_dev = w_in.shape[0]
    reach = exp_dev * capacity
    parts = 2 if chan_dev % 16 == 0 and blocks % 16 == 0 else 1
    route_row = routes.reshape(1, len_dev)
    index_rows = gate_index.reshape(len_dev, TASKS).T
    gate_cols = gate_weight.transpose(0, 2, 1).reshape(TASKS * EXPERTS, channels)

    slot, size = slots_of(route_row, exp_dev, reach)
    totals = jnp.sum(size[0, :EXPERTS].reshape(1, n_seq, exp_dev), -1)
    all_in = lax.all_gather(w_in, "batch", axis=0, tiled=False)
    rows = events.reshape(len_dev, channels)

    length = len_dev * n_seq
    filt = spectral_filter.transpose(0, 2, 1).reshape(2, chan_dev, INNER, length // INNER)
    chan_part = chan_dev // parts
    returned = []
    for part in range(parts):
        turned = turn(rows, size, chan_dev, parts, part, *([filt] if part else []))
        history = lax.all_to_all(turned, "seq", split_axis=0, concat_axis=0, tiled=True)
        history = history.reshape(n_seq, -1, blocks, INNER)
        if part == 0:
            with_counts = history
        if blocks % 16:
            merged = history[:, :chan_part].transpose(1, 0, 2, 3)
            merged = merged.reshape(1, chan_part, n_seq * blocks, INNER)
            summed = spectral(merged, filt, part, chan_part)
            summed = summed.reshape(chan_part, n_seq, blocks, INNER).transpose(1, 0, 2, 3)
        else:
            summed = spectral(history, filt, part, chan_part)
        summed = summed.reshape(n_seq, chan_part * blocks, INNER)
        first = summed if part == 0 else first
        returned.append(
            lax.all_to_all(summed, "seq", split_axis=0, concat_axis=0, tiled=True)
        )

    heights = tier_heights(reach)
    tail, counts = tier_of(with_counts, chan_part, exp_dev, heights, channels, first)
    inverse = inverse_of(slot, n_seq * reach, first)
    hid = w_out.shape[1]
    with_tier = jnp.concatenate([w_out.reshape(exp_dev * hid, channels), tail], 0)
    all_out = lax.all_gather(with_tier, "batch", axis=0, tiled=False)
    tier = jnp.max(all_out[:, exp_dev * hid, 0].astype(F32)).astype(jnp.int32)
    own = lax.dynamic_slice(counts, (0, lax.axis_index("seq") * exp_dev), (n_seq, exp_dev))
    ahead = jnp.arange(exp_dev)[:, None] > jnp.arange(exp_dev)[None, :]
    start = jnp.sum(jnp.where(ahead[None], own[:, None, :], 0), -1)

    def mixture(height, returned, slot, inverse, totals, start, own, all_in, all_out):
        chunks = 2 if height % (2 * ROWS) == 0 else 1
        chunk_rows = height // chunks
        owner, local = slot // reach, slot % reach
        chunk_of = local // chunk_rows
        place = (chunk_of * n_seq + owner) * chunk_rows + local % chunk_rows
        *outgoing, gates = norm_and_send(
            returned,
            ln_gain.reshape(1, channels),
            gate_cols,
            route_row,
            index_rows,
            place,
            gate_table,
            n_seq * height,
            chunks,
        )
        results = []
        for chunk, rows in enumerate(outgoing):
            arrived = lax.all_to_all(
                rows.reshape(n_seq, chunk_rows, channels),
                "seq", split_axis=0, concat_axis=0, tiled=True,
            )
            done = experts(arrived, all_in, all_out, start, own, chunk, chunks, capacity)
            back = lax.all_to_all(done, "seq", split_axis=0, concat_axis=0, tiled=True)
            back = back.reshape(n_seq * chunk_rows, channels)
            if chunk < chunks - 1:
                results = put_back(results, back, inverse, totals, chunk, reach, len_dev)
        return finish(results, back, gates, inverse, totals, chunks - 1, reach)

    branches = [functools.partial(mixture, height) for height in heights]
    task_out = lax.switch(
        tier, branches, returned, slot, inverse, totals, start, own, all_in, all_out
    )
    return task_out.reshape(TASKS, 1, len_dev, user_count, channels)


def tier_heights(reach):
    if reach % 1024:
        return [reach]
    return [reach // 32 * share for share in (21, 22, 23, 24, 25, 26, 28, 32)]


def solution(mesh):
    in_specs = (
        P("batch", "seq", None, None),
        P(None, None, "seq"),
        P(),
        P("seq", "batch", None),
        P("seq", "batch", None),
        P(),
        P(),
        P("batch", "seq", None, None),
        P("batch", "seq", None, None),
    )
    out_specs = P(None, "batch", "seq", None, None)
    return jax.shard_map(
        on_device, mesh=mesh, in_specs=in_specs, out_specs=out_specs, check_vma=False
    )
```
